128 devices in a mesh: region: 16 (over z, y), sub: 8 (over x, core).
Axes of the slice: x: 4, y: 4, z: 4, core: 2. Of those that a mesh axis runs over, the one named last changes fastest.
Arguments:
- mass_field: float32 [96, 393216], P(None, ('region', 'sub')), may hold values from -6 to 6
- normal_wind: float32 [96, 589824], P(None, ('region', 'sub')), may hold values from -6 to 6
- tracer_ratio: float32 [96, 393216], P(None, ('region', 'sub')), may hold values from 0.2 to 2
- gradient_weights: float32 [4608, 3, 128, 128], P(('region', 'sub')), may hold values from -0.3125 to 0.3125
- divergence_weights: float32 [3072, 4, 128, 128], P(('region', 'sub')), may hold values from -0.25 to 0.25
- vertical_inverse: float32 [3072, 96, 96], P(('region', 'sub')), may hold values from -1 to 1
- gradient_pattern: int32 [4608, 3], P(('region', 'sub')), may hold values from 0 to 39, as said below
- divergence_pattern: int32 [3072, 4], P(('region', 'sub')), may hold values from 0 to 51, as said below
- edge_cells: int32 [2, 851968], P(None, ('region', 'sub')), may hold values from 0 to 6143, as said below
- cell_sends: int32 [128, 16], P(('region', 'sub')), may hold values from -1 to 23, as said below
- edge_sends: int32 [128, 16], P(('region', 'sub')), may hold values from -1 to 35, as said below
- wide_sends: int32 [128, 24], P(('region', 'sub')), may hold values from -1 to 23, as said below
Outputs:
- mass_final: float32 [96, 393216], P(None, ('region', 'sub'))
- wind_final: float32 [96, 589824], P(None, ('region', 'sub'))
- tracer_final: float32 [96, 393216], P(None, ('region', 'sub'))
The draws below stay inside these ranges and needn't reach their ends.
Inputs may be any that keep to these rules, and one draw needn't show every extreme that they name: `cell_sends`: -1 marks an empty slot, any other entry one of the device's own 24 blocks; every device sends nothing to its own sub-region nor past the first or last region, fills all slots for one other sub-region and for one neighbouring region, and at least one slot for every other peer that exists. `edge_sends`: as for cell_sends, with blocks of the device's own 36 edge blocks. `wide_sends`: as for cell_sends, with the tracer's 24 blocks. `gradient_pattern`: the first entry of each row is one of the device's own blocks; every block of the extended cell set appears somewhere on each device. `divergence_pattern`: every block of the extended edge set appears somewhere on each device. `edge_cells`: cell numbers within the device's extended tracer set; every such cell appears on each device.
All inputs are finite; a program needn't handle non-finite values.
Results may differ from the reference program's by a relative error of at most 0.0003.
Values sent between devices are 32-bit elements; how exact they have to be, the bound alone decides.
No kernel may reach another device: no remote copies, remote signals or barrier semaphores. Data moves between devices by JAX's collectives and lax.ppermute only.
A program may use at most 128 MiB of HBM per device.

```python
import math
import jax
import jax.numpy as jnp
from jax import lax

BLOCK = 128
LEV = 96
NB = 24
NE = 36
KG = 3
KD = 4
SS = 1
SR = 4
ES = 1
ER = 4
WS = 1
WR = 8
SUBSTEPS = 5
CELLS = 393216
EDGES = 589824
BLOCKS = 3072
EBLOCKS = 4608
EXTC = 40
EXTE = 52
EXTW = 48
N_REGION = 16
N_SUB = 8


def send_lists(key, per_peer, per_side, own_count):
    devices = N_REGION * N_SUB
    subkeys = jax.random.split(key, 6)
    device_ids = jnp.arange(devices, dtype=jnp.int32)
    sub_of = device_ids % N_SUB
    region_of = device_ids // N_SUB
    entries = jax.random.randint(subkeys[0], (devices, N_SUB, per_peer), 0, own_count, dtype=jnp.int32)
    counts = jax.random.randint(subkeys[1], (devices, N_SUB), 1, per_peer + 1, dtype=jnp.int32)
    full_peer = (sub_of + jax.random.randint(subkeys[2], (devices,), 1, N_SUB, dtype=jnp.int32)) % N_SUB
    peer_ids = jnp.arange(N_SUB, dtype=jnp.int32)
    counts = jnp.where(peer_ids[None, :] == full_peer[:, None], per_peer, counts)
    counts = jnp.where(peer_ids[None, :] == sub_of[:, None], 0, counts)
    slot_ids = jnp.arange(per_peer, dtype=jnp.int32)
    lateral = jnp.where(slot_ids[None, None, :] < counts[:, :, None], entries, -1).reshape(devices, N_SUB * per_peer)
    side_entries = jax.random.randint(subkeys[3], (devices, 2, per_side), 0, own_count, dtype=jnp.int32)
    side_counts = jax.random.randint(subkeys[4], (devices, 2), 1, per_side + 1, dtype=jnp.int32)
    full_side = jax.random.randint(subkeys[5], (devices,), 0, 2, dtype=jnp.int32)
    full_side = jnp.where(region_of == 0, 0, jnp.where(region_of == N_REGION - 1, 1, full_side))
    side_ids = jnp.arange(2, dtype=jnp.int32)
    side_counts = jnp.where(side_ids[None, :] == full_side[:, None], per_side, side_counts)
    side_counts = jnp.where((side_ids[None, :] == 0) & (region_of[:, None] == N_REGION - 1), 0, side_counts)
    side_counts = jnp.where((side_ids[None, :] == 1) & (region_of[:, None] == 0), 0, side_counts)
    side_slots = jnp.arange(per_side, dtype=jnp.int32)
    side_list = jnp.where(side_slots[None, None, :] < side_counts[:, :, None], side_entries, -1).reshape(devices, 2 * per_side)
    return jnp.concatenate([lateral, side_list], axis=1).astype(jnp.int32)


def draw_cell_sends(key, part):
    key = jax.random.fold_in(key, 11)
    return send_lists(key, SS, SR, NB)


def draw_edge_sends(key, part):
    key = jax.random.fold_in(key, 12)
    return send_lists(key, ES, ER, NE)


def draw_wide_sends(key, part):
    key = jax.random.fold_in(key, 13)
    return send_lists(key, WS, WR, NB)


def draw_gradient_pattern(key, part):
    key = jax.random.fold_in(key, 21)
    devices = N_REGION * N_SUB
    subkeys = jax.random.split(key, devices + 1)
    own_part = jax.random.randint(subkeys[0], (devices, NE, 1), 0, NB, dtype=jnp.int32)

    def spread(one_key):
        return (jax.random.permutation(one_key, NE * (KG - 1)).astype(jnp.int32) % EXTC).reshape(NE, KG - 1)
    remote_part = jax.vmap(spread)(subkeys[1:])
    return jnp.concatenate([own_part, remote_part], axis=2).reshape(devices * NE, KG).astype(jnp.int32)


def draw_divergence_pattern(key, part):
    key = jax.random.fold_in(key, 22)
    devices = N_REGION * N_SUB
    subkeys = jax.random.split(key, devices)

    def spread(one_key):
        return (jax.random.permutation(one_key, NB * KD).astype(jnp.int32) % EXTE).reshape(NB, KD)
    return jax.vmap(spread)(subkeys).reshape(devices * NB, KD).astype(jnp.int32)


def draw_edge_cells(key, part):
    key = jax.random.fold_in(key, 23)
    devices = N_REGION * N_SUB
    subkeys = jax.random.split(key, devices)

    def spread(one_key):
        return (jax.random.permutation(one_key, 2 * EXTE * BLOCK).astype(jnp.int32) % (EXTW * BLOCK)).reshape(2, EXTE * BLOCK)
    stacked = jax.vmap(spread)(subkeys)
    return jnp.transpose(stacked, (1, 0, 2)).reshape(2, devices * EXTE * BLOCK).astype(jnp.int32)


def draw_vertical_inverse(key, part):
    key = jax.random.fold_in(key, 41)
    first_key, second_key = jax.random.split(key)
    shape = (BLOCKS, LEV, LEV)
    uniform_diag = jax.random.uniform(first_key, (BLOCKS, LEV), jnp.float32)
    diagonal = 0.4 * jnp.exp(uniform_diag * math.log(2.5))
    off_part = jax.random.truncated_normal(second_key, -4.0, 4.0, shape, jnp.float32) * (0.6 / math.sqrt(LEV))
    identity = jnp.eye(LEV, dtype=jnp.float32)
    return (off_part * (1.0 - identity[None]) + identity[None] * diagonal[:, :, None]).astype(jnp.float32)


def steps_of(rng, shape, shards, least, top_value):
    def one(dim, shards_of):
        steps = jax.random.uniform(jax.random.fold_in(jax.random.fold_in(rng, 6), dim), (shards_of,), jnp.float32, least / len(shards), top_value / len(shards))
        return jnp.repeat(jnp.exp(steps), shape[dim] // shards_of).reshape((-1,) + (1,) * (len(shape) - dim - 1))

    gain = one(*shards[0])
    for cut in shards[1:]:
        gain = gain * one(*cut)
    return gain


def normal_values(rng, extent, deviation, most, cuts=(), kind=jnp.bfloat16):
    values = jax.random.normal(rng, extent, jnp.float32) * deviation
    if len(cuts) > 0:
        values = steps_of(rng, extent, cuts, -0.22, 0.18) * values
    return jnp.clip(values, min=-most, max=most).astype(kind)


def setup_inputs(seed: int = 0) -> dict:
    seeds = jax.random.split(jax.random.key(seed), 13)
    mass_field = normal_values(seeds[0], (LEV, CELLS), 1.0, 6.0, ((1, 128),), jnp.float32)
    normal_wind = normal_values(seeds[1], (LEV, EDGES), 1.0, 6.0, ((1, 128),), jnp.float32)
    tracer_ratio = jnp.clip(0.2 + 1.8 * jax.random.uniform(seeds[2], (LEV, CELLS), jnp.float32) ** steps_of(seeds[2], (LEV, CELLS), ((1, 128),), -0.2, 0.2), 0.2, 2.0)
    gradient_weights = normal_values(seeds[3], (EBLOCKS, KG, BLOCK, BLOCK), (KG * BLOCK) ** -0.5, 0.3125, ((0, 128),), jnp.float32)
    divergence_weights = normal_values(seeds[4], (BLOCKS, KD, BLOCK, BLOCK), (KD * BLOCK) ** -0.5, 0.25, ((0, 128),), jnp.float32)
    vertical_inverse = draw_vertical_inverse(jax.random.fold_in(seeds[12], 71), 0)
    gradient_pattern = draw_gradient_pattern(jax.random.fold_in(seeds[12], 71), 0)
    divergence_pattern = draw_divergence_pattern(jax.random.fold_in(seeds[12], 71), 0)
    edge_cells = draw_edge_cells(jax.random.fold_in(seeds[12], 71), 0)
    cell_sends = draw_cell_sends(jax.random.fold_in(seeds[12], 71), 0)
    edge_sends = draw_edge_sends(jax.random.fold_in(seeds[12], 71), 0)
    wide_sends = draw_wide_sends(jax.random.fold_in(seeds[12], 71), 0)
    return dict(mass_field=mass_field, normal_wind=normal_wind, tracer_ratio=tracer_ratio, gradient_weights=gradient_weights, divergence_weights=divergence_weights, vertical_inverse=vertical_inverse, gradient_pattern=gradient_pattern, divergence_pattern=divergence_pattern, edge_cells=edge_cells, cell_sends=cell_sends, edge_sends=edge_sends, wide_sends=wide_sends)


time_step = 0.25
tracer_step = 0.5


def extend(field, send_list, per_peer, per_side):
    levels = field.shape[0]
    devices = N_REGION * N_SUB
    blocks = field.reshape(levels, devices, -1, BLOCK)
    is_live = (send_list >= 0).astype(field.dtype)
    picked_blocks = jax.vmap(lambda own_blocks, wanted: jnp.take(own_blocks, wanted, axis=1), in_axes=(1, 0), out_axes=1)(blocks, jnp.maximum(send_list, 0).astype(jnp.int32))
    picked_blocks = picked_blocks * is_live[None, :, :, None]
    split_at = N_SUB * per_peer
    lateral = picked_blocks[:, :, :split_at].reshape(levels, N_REGION, N_SUB, N_SUB, per_peer, BLOCK)
    lateral_in = jnp.swapaxes(lateral, 2, 3).reshape(levels, devices, split_at, BLOCK)
    to_next = picked_blocks[:, :, split_at:split_at + per_side].reshape(levels, N_REGION, N_SUB, per_side, BLOCK)
    to_prev = picked_blocks[:, :, split_at + per_side:].reshape(levels, N_REGION, N_SUB, per_side, BLOCK)
    zero_rim = jnp.zeros((levels, 1, N_SUB, per_side, BLOCK), field.dtype)
    from_prev = jnp.concatenate([zero_rim, to_next[:, :-1]], axis=1).reshape(levels, devices, per_side, BLOCK)
    from_next = jnp.concatenate([to_prev[:, 1:], zero_rim], axis=1).reshape(levels, devices, per_side, BLOCK)
    return jnp.concatenate([blocks, lateral_in, from_prev, from_next], axis=2)


def block_product(rimmed, pattern, weights, targets, width):
    levels = rimmed.shape[0]
    devices = N_REGION * N_SUB
    pattern_dev = pattern.reshape(devices, targets, width)
    weights_dev = weights.reshape(devices, targets, width, BLOCK, BLOCK)

    def per_device(operands):
        rim_dev, pattern_one, weights_one = operands
        gathered = rim_dev[:, pattern_one]
        return jnp.einsum('lnkc,nkcj->lnj', gathered, weights_one, precision=lax.Precision.HIGHEST)

    result = lax.map(per_device, (jnp.moveaxis(rimmed, 1, 0), pattern_dev, weights_dev))
    return jnp.moveaxis(result, 0, 1).reshape(levels, -1)


def vertical(pending, inverse):
    levels = pending.shape[0]
    shaped = pending.reshape(levels, inverse.shape[0], BLOCK)
    return jnp.einsum('blm,mbj->lbj', inverse, shaped, precision=lax.Precision.HIGHEST).reshape(levels, -1)


def reference(mass_field, normal_wind, tracer_ratio, gradient_weights, divergence_weights, vertical_inverse, gradient_pattern, divergence_pattern, edge_cells, cell_sends, edge_sends, wide_sends):
    levels = mass_field.shape[0]
    devices = N_REGION * N_SUB
    mass_now = mass_field
    wind_now = normal_wind
    wind_total = jnp.zeros((levels, devices, EXTE, BLOCK), jnp.float32)
    for substep in range(SUBSTEPS):
        cells_rimmed = extend(mass_now, cell_sends, SS, SR)
        wind_now = wind_now - time_step * block_product(cells_rimmed, gradient_pattern, gradient_weights, NE, KG)
        edges_rimmed = extend(wind_now, edge_sends, ES, ER)
        wind_total = wind_total + edges_rimmed
        pending = mass_now - time_step * block_product(edges_rimmed, divergence_pattern, divergence_weights, NB, KD)
        mass_now = vertical(pending, vertical_inverse)
    tracer_rimmed = extend(tracer_ratio, wide_sends, WS, WR).reshape(levels, devices, EXTW * BLOCK)
    links = edge_cells.reshape(2, devices, EXTE * BLOCK)

    def edge_average(cells_dev, first_cell, second_cell):
        return 0.5 * (jnp.take(cells_dev, first_cell, axis=1) + jnp.take(cells_dev, second_cell, axis=1))

    edge_tracer = jax.vmap(edge_average, in_axes=(1, 0, 0), out_axes=1)(tracer_rimmed, links[0], links[1])
    tracer_flux = (wind_total.reshape(levels, devices, EXTE * BLOCK) / SUBSTEPS) * edge_tracer
    tracer_flux = tracer_flux.reshape(levels, devices, EXTE, BLOCK)
    tracer_final = tracer_ratio - tracer_step * block_product(tracer_flux, divergence_pattern, divergence_weights, NB, KD)
    return mass_now, wind_now, tracer_final
```

```python
import functools

import numpy as np
import jax
import jax.numpy as jnp
from jax import lax
from jax.experimental import pallas as pl
from jax.experimental.pallas import tpu as pltpu
from jax.sharding import PartitionSpec as P

BLOCK = 128
LEV = 96
NB = 24
NE = 36
KG = 3
KD = 4
SR = 4
ER = 4
WR = 8
SUBSTEPS = 5
N_REGION = 16
N_CHIP = 4
N_SUB = 8
LAT = 8

time_step = 0.25
tracer_step = 0.5

BF = jnp.bfloat16
F32 = jnp.float32

ALONG = [(2 * x + c, 2 * ((x + (1 if c == 0 else 3)) % 4) + c) for x in range(4) for c in range(2)]
ACROSS = [(2 * x + c, 2 * ((x + 2) % 4) + c) for x in range(4) for c in range(2)]
MATES = [(s, s ^ 1) for s in range(8)]


def send_order():
    rows = []
    for s in range(N_SUB):
        x, c = divmod(s, 2)
        mine = (x + (1 if c == 0 else 3)) % 4
        other = (x + (3 if c == 0 else 1)) % 4
        far = (x + 2) % 4
        o = 1 - c
        rows.append([2 * x + o, 2 * other + o, 2 * other + c, 2 * mine + c, 2 * mine + o, 2 * far + c, 2 * far + o])
    return np.array(rows, np.int32)


def lateral_place():
    rows = []
    for s in range(N_SUB):
        x, c = divmod(s, 2)
        back = 3 if c == 0 else 1
        row = []
        for p in range(N_SUB):
            px, pc = divmod(p, 2)
            d = (px - x) % 4
            same = pc == c
            if d == 0:
                row.append(7 if same else 0)
            elif d == back:
                row.append(1 if same else 2)
            elif d == 2:
                row.append(3 if same else 6)
            else:
                row.append(5 if same else 4)
        rows.append(row)
    return np.array(rows, np.int32)


def place_table(own, side):
    lat = lateral_place()
    rows = [
        np.concatenate([np.arange(own), own + lat[s], own + LAT + np.arange(2 * side)])
        for s in range(N_SUB)
    ]
    return np.stack(rows).astype(np.int32)


ORDER = send_order()


def row_of(table):
    sub = lax.axis_index("sub")
    return lax.dynamic_slice(jnp.asarray(table), (sub, 0), (1, table.shape[1]))[0]


def ring(v, step):
    return lax.ppermute(v, "region", [(s, (s + step) % N_REGION) for s in range(N_REGION)])


def exchange(sends):
    pre, along, across, to_next, to_prev = sends
    from_prev = ring(to_next, 1)
    from_next = ring(to_prev, -1)
    pre_in = lax.ppermute(pre, "sub", MATES)
    along_in = lax.ppermute(jnp.concatenate([along, pre_in[1:]], axis=0), "sub", ALONG)
    across_in = lax.ppermute(across, "sub", ACROSS)
    post = jnp.concatenate([along_in[1:2], along_in[3:4], across_in[1:2]], axis=0)
    post_in = lax.ppermute(post, "sub", MATES)
    return pre_in, along_in, across_in, post_in, from_prev, from_next


def two_parts(x):
    hi = x.astype(BF)
    lo = (x - hi.astype(F32)).astype(BF)
    return hi, lo


def split_kernel(w_ref, o_ref):
    hi, lo = two_parts(w_ref[...])
    o_ref[:, :, :BLOCK] = hi
    o_ref[:, :, BLOCK:] = lo


def split_weights(weights, per_step):
    n = weights.shape[0] * weights.shape[1]
    flat = weights.reshape(n, BLOCK, BLOCK)
    return pl.pallas_call(
        split_kernel,
        grid=(n // per_step,),
        in_specs=[pl.BlockSpec((per_step, BLOCK, BLOCK), lambda i: (i, 0, 0))],
        out_specs=pl.BlockSpec((per_step, BLOCK, 2 * BLOCK), lambda i: (i, 0, 0)),
        out_shape=jax.ShapeDtypeStruct((n, BLOCK, 2 * BLOCK), BF),
        compiler_params=pltpu.CompilerParams(vmem_limit_bytes=32 << 20),
        cost_estimate=pl.CostEstimate(flops=n * BLOCK * BLOCK * 4, bytes_accessed=n * BLOCK * BLOCK * 8, transcendentals=0),
        name="split_weights",
    )(flat)


RIM = (("pre", 0), ("along", 0), ("along", 2), ("across", 0), ("post", 0), ("post", 1), ("post", 2))


def rim_blocks(rim, side):
    pre, along, across, post, prev, nxt = rim
    by_name = dict(pre=pre, along=along, across=across, post=post)
    blocks = [(j, by_name[name], i) for j, (name, i) in enumerate(RIM)]
    blocks += [(LAT + i, prev, i) for i in range(side)]
    blocks += [(LAT + side + i, nxt, i) for i in range(side)]
    return blocks


def store_parts(ext, slot, x):
    hi, lo = two_parts(x)
    ext[slot, :LEV, :] = hi
    ext[slot, LEV:, :] = lo


def block_at(ref, b):
    return ref[:, pl.ds(pl.multiple_of(b * BLOCK, BLOCK), BLOCK)]


def fill_extended(ext, own_ref, own, rim, side):
    def one(b, _):
        store_parts(ext, b, block_at(own_ref, b))
        return 0

    lax.fori_loop(0, own, one, 0, unroll=4)
    for j, ref, i in rim_blocks(rim, side):
        store_parts(ext, own + j, ref[i])
    ext[own + LAT - 1] = jnp.zeros((2 * LEV, BLOCK), BF)


def target_product(ext, pattern, place, w_ref, base, local, width):
    xs = [ext[place[pattern[(base + local) * width + k]]] for k in range(width)]
    x = jnp.concatenate(xs, axis=1)
    w = w_ref[local * width : (local + 1) * width].reshape(width * BLOCK, 2 * BLOCK)
    y = jnp.dot(x, w, preferred_element_type=F32)
    return (y[:LEV, :BLOCK] + y[LEV:, :BLOCK]) + (y[:LEV, BLOCK:] + y[LEV:, BLOCK:])


def pick(source, entry):
    live = (entry >= 0).astype(F32)
    return source(jnp.maximum(entry, 0)) * live


def fill_sends(sends, send_list, order, source, side):
    pre, along, across, to_next, to_prev = sends
    for j in range(3):
        pre[j] = pick(source, send_list[order[j]])
    for j in range(2):
        along[j] = pick(source, send_list[order[3 + j]])
        across[j] = pick(source, send_list[order[5 + j]])
    for j in range(side):
        to_next[j] = pick(source, send_list[LAT + j])
        to_prev[j] = pick(source, send_list[LAT + side + j])


def send_shapes(side):
    return [jax.ShapeDtypeStruct((n, LEV, BLOCK), F32) for n in (3, 2, 2, side, side)]


def whole(shape):
    return pl.BlockSpec(shape, lambda *_: (0,) * len(shape))


def send_specs(side):
    return [whole((n, LEV, BLOCK)) for n in (3, 2, 2, side, side)]


def rim_specs(side):
    return [whole((n, LEV, BLOCK)) for n in (3, 4, 2, 3, side, side)]


def first_kernel(send_list, order, field_ref, *sends, side):
    fill_sends(sends, send_list, order, lambda b: block_at(field_ref, b), side)


def first_sends(field, send_list, order, side):
    return pl.pallas_call(
        functools.partial(first_kernel, side=side),
        grid_spec=pltpu.PrefetchScalarGridSpec(
            num_scalar_prefetch=2,
            grid=(1,),
            in_specs=[whole(field.shape)],
            out_specs=send_specs(side),
        ),
        out_shape=send_shapes(side),
        compiler_params=pltpu.CompilerParams(vmem_limit_bytes=32 << 20),
        name="first_sends",
    )(send_list, order, field)


G_STEP = 6


def gradient_kernel(pattern, place, send_list, order, mass_ref, wind_ref, w_ref, *refs):
    rim, out_ref, sends, ext, keep = refs[:6], refs[6], refs[7:12], refs[12], refs[13]
    step = pl.program_id(0)

    @pl.when(step == 0)
    def _():
        fill_extended(ext, mass_ref, NB, rim, SR)

    base = step * G_STEP
    for j in range(G_STEP):
        p = target_product(ext, pattern, place, w_ref, base, j, KG)
        new = wind_ref[:, j * BLOCK : (j + 1) * BLOCK] - time_step * p
        out_ref[:, j * BLOCK : (j + 1) * BLOCK] = new
        keep[base + j] = new

    @pl.when(step == NE // G_STEP - 1)
    def _():
        fill_sends(sends, send_list, order, lambda b: keep[b], ER)


def gradient(info, mass, wind, weights, rim):
    steps = NE // G_STEP
    out = pl.pallas_call(
        gradient_kernel,
        grid_spec=pltpu.PrefetchScalarGridSpec(
            num_scalar_prefetch=4,
            grid=(steps,),
            in_specs=[
                whole(mass.shape),
                pl.BlockSpec((LEV, G_STEP * BLOCK), lambda i, *_: (0, i)),
                pl.BlockSpec((G_STEP * KG, BLOCK, 2 * BLOCK), lambda i, *_: (i, 0, 0)),
                *rim_specs(SR),
            ],
            out_specs=[pl.BlockSpec((LEV, G_STEP * BLOCK), lambda i, *_: (0, i)), *send_specs(ER)],
            scratch_shapes=[
                pltpu.VMEM((NB + LAT + 2 * SR, 2 * LEV, BLOCK), BF),
                pltpu.VMEM((NE, LEV, BLOCK), F32),
            ],
        ),
        out_shape=[jax.ShapeDtypeStruct(wind.shape, F32), *send_shapes(ER)],
        compiler_params=pltpu.CompilerParams(vmem_limit_bytes=40 << 20),
        name="gradient",
    )(*info, mass, wind, weights, *rim)
    return out[0], out[1:]


D_STEP = 4


def divergence_kernel(pattern, place, send_list, order, wind_ref, mass_ref, w_ref, inv_ref, *refs):
    rim, out_ref, sends, ext, keep = refs[:6], refs[6], refs[7:12], refs[12], refs[13]
    step = pl.program_id(0)

    @pl.when(step == 0)
    def _():
        fill_extended(ext, wind_ref, NE, rim, ER)

    base = step * D_STEP
    for j in range(D_STEP):
        p = target_product(ext, pattern, place, w_ref, base, j, KD)
        pending = mass_ref[:, j * BLOCK : (j + 1) * BLOCK] - time_step * p
        v_hi, v_lo = two_parts(inv_ref[j])
        p_hi, p_lo = two_parts(pending)
        y = jnp.dot(jnp.concatenate([v_hi, v_lo], axis=0), jnp.concatenate([p_hi, p_lo], axis=1), preferred_element_type=F32)
        new = (y[:LEV, :BLOCK] + y[LEV:, :BLOCK]) + (y[:LEV, BLOCK:] + y[LEV:, BLOCK:])
        out_ref[:, j * BLOCK : (j + 1) * BLOCK] = new
        keep[base + j] = new

    @pl.when(step == NB // D_STEP - 1)
    def _():
        fill_sends(sends, send_list, order, lambda b: keep[b], SR)


def divergence(info, wind, mass, weights, inverse, rim):
    steps = NB // D_STEP
    out = pl.pallas_call(
        divergence_kernel,
        grid_spec=pltpu.PrefetchScalarGridSpec(
            num_scalar_prefetch=4,
            grid=(steps,),
            in_specs=[
                whole(wind.shape),
                pl.BlockSpec((LEV, D_STEP * BLOCK), lambda i, *_: (0, i)),
                pl.BlockSpec((D_STEP * KD, BLOCK, 2 * BLOCK), lambda i, *_: (i, 0, 0)),
                pl.BlockSpec((D_STEP, LEV, LEV), lambda i, *_: (i, 0, 0)),
                *rim_specs(ER),
            ],
            out_specs=[pl.BlockSpec((LEV, D_STEP * BLOCK), lambda i, *_: (0, i)), *send_specs(SR)],
            scratch_shapes=[
                pltpu.VMEM((NE + LAT + 2 * ER, 2 * LEV, BLOCK), BF),
                pltpu.VMEM((NB, LEV, BLOCK), F32),
            ],
        ),
        out_shape=[jax.ShapeDtypeStruct(mass.shape, F32), *send_shapes(SR)],
        compiler_params=pltpu.CompilerParams(vmem_limit_bytes=40 << 20),
        name="divergence",
    )(*info, wind, mass, weights, inverse, *rim)
    return out[0], out[1:]


T_STEP = 13
ROWS_AT_ONCE = 16


def turned(x):
    return jnp.transpose(x, (1, 0))


def table_kernel(tracer_ref, *refs):
    rim, table_ref = refs[:6], refs[6]

    def put(slot, x):
        padded = jnp.concatenate([x, jnp.zeros((BLOCK - LEV, BLOCK), F32)], axis=0)
        start = slot * BLOCK if isinstance(slot, int) else pl.multiple_of(slot * BLOCK, BLOCK)
        table_ref[pl.ds(start, BLOCK), :] = turned(padded)

    def one(b, _):
        put(b, block_at(tracer_ref, b))
        return 0

    lax.fori_loop(0, NB, one, 0, unroll=2)
    for j, ref, i in rim_blocks(rim, WR):
        put(NB + j, ref[i])
    put(NB + LAT - 1, jnp.zeros((LEV, BLOCK), F32))


def tracer_table(tracer, rim):
    cells = (NB + LAT + 2 * WR) * BLOCK
    return pl.pallas_call(
        table_kernel,
        grid=(1,),
        in_specs=[whole(tracer.shape), *rim_specs(WR)],
        out_specs=whole((cells, BLOCK)),
        out_shape=jax.ShapeDtypeStruct((cells, BLOCK), F32),
        compiler_params=pltpu.CompilerParams(vmem_limit_bytes=32 << 20),
        cost_estimate=pl.CostEstimate(flops=0, bytes_accessed=8 << 20, transcendentals=0),
        name="tracer_table",
    )(tracer, *rim)


def edge_tracer_kernel(cells, table_ref, out_ref, rows, *, first):
    count = T_STEP * BLOCK

    def block(e, _):
        def some(i, _):
            at = e * BLOCK + i * ROWS_AT_ONCE
            for j in range(ROWS_AT_ONCE):
                a = table_ref[pl.ds(cells[at + j], 1), :]
                b = table_ref[pl.ds(cells[count + at + j], 1), :]
                rows[pl.ds(i * ROWS_AT_ONCE + j, 1), :] = a + b
            return 0

        lax.fori_loop(0, BLOCK // ROWS_AT_ONCE, some, 0)
        out_ref[e] = 0.5 * turned(rows[...])[:LEV]
        return 0

    lax.fori_loop(0, T_STEP, block, 0)


def edge_tracer_part(table, cells, first):
    return pl.pallas_call(
        functools.partial(edge_tracer_kernel, first=first),
        grid_spec=pltpu.PrefetchScalarGridSpec(
            num_scalar_prefetch=1,
            grid=(1,),
            in_specs=[whole(table.shape)],
            out_specs=whole((T_STEP, LEV, BLOCK)),
            scratch_shapes=[pltpu.VMEM((BLOCK, BLOCK), F32)],
        ),
        out_shape=jax.ShapeDtypeStruct((T_STEP, LEV, BLOCK), F32),
        compiler_params=pltpu.CompilerParams(vmem_limit_bytes=32 << 20),
        cost_estimate=pl.CostEstimate(flops=0, bytes_accessed=16 << 20, transcendentals=0),
        name="edge_tracer",
    )(cells, table)


def transport_kernel(pattern, place, total_ref, tracer_ref, w_ref, edge_ref, *refs):
    rim, out_ref, ext = refs[:6], refs[6], refs[7]
    step = pl.program_id(0)

    @pl.when(step == 0)
    def _():
        def one(b, _):
            store_parts(ext, b, (block_at(total_ref, b) / SUBSTEPS) * edge_ref[b])
            return 0

        lax.fori_loop(0, NE, one, 0, unroll=4)
        for j, ref, i in rim_blocks(rim, ER):
            store_parts(ext, NE + j, (ref[i] / SUBSTEPS) * edge_ref[NE + j])
        ext[NE + LAT - 1] = jnp.zeros((2 * LEV, BLOCK), BF)

    base = step * D_STEP
    for j in range(D_STEP):
        p = target_product(ext, pattern, place, w_ref, base, j, KD)
        out_ref[:, j * BLOCK : (j + 1) * BLOCK] = tracer_ref[:, j * BLOCK : (j + 1) * BLOCK] - tracer_step * p


def transport(pattern, place, total, tracer, weights, edge_tracer, rim):
    steps = NB // D_STEP
    return pl.pallas_call(
        transport_kernel,
        grid_spec=pltpu.PrefetchScalarGridSpec(
            num_scalar_prefetch=2,
            grid=(steps,),
            in_specs=[
                whole(total.shape),
                pl.BlockSpec((LEV, D_STEP * BLOCK), lambda i, *_: (0, i)),
                pl.BlockSpec((D_STEP * KD, BLOCK, 2 * BLOCK), lambda i, *_: (i, 0, 0)),
                whole(edge_tracer.shape),
                *rim_specs(ER),
            ],
            out_specs=pl.BlockSpec((LEV, D_STEP * BLOCK), lambda i, *_: (0, i)),
            scratch_shapes=[pltpu.VMEM((NE + LAT + 2 * ER, 2 * LEV, BLOCK), BF)],
        ),
        out_shape=jax.ShapeDtypeStruct(tracer.shape, F32),
        compiler_params=pltpu.CompilerParams(vmem_limit_bytes=40 << 20),
        name="transport",
    )(pattern, place, total, tracer, weights, edge_tracer, *rim)


def edge_order():
    place = place_table(NE, ER)
    return np.argsort(place, axis=1).astype(np.int32)


def body(
    mass_field,
    normal_wind,
    tracer_ratio,
    gradient_weights,
    divergence_weights,
    vertical_inverse,
    gradient_pattern,
    divergence_pattern,
    edge_cells,
    cell_sends,
    edge_sends,
    wide_sends,
):
    order = row_of(ORDER)
    cell_place = row_of(place_table(NB, SR))
    edge_place = row_of(place_table(NE, ER))
    wide_place = row_of(place_table(NB, WR))
    cell_list, edge_list, wide_list = cell_sends[0], edge_sends[0], wide_sends[0]
    g_pattern = gradient_pattern.reshape(-1)
    d_pattern = divergence_pattern.reshape(-1)

    rim = exchange(first_sends(mass_field, cell_list, order, SR))
    g_weights = split_weights(gradient_weights, 18)
    d_weights = split_weights(divergence_weights, 16)

    held = row_of(edge_order())
    by_block = jnp.take(edge_cells.reshape(2, -1, BLOCK), held, axis=1)
    wanted = by_block // BLOCK
    lateral = (wanted >= NB) & (wanted < NB + LAT)
    place_lat = jnp.zeros_like(wanted)
    for p in range(LAT):
        place_lat = jnp.where(wanted == NB + p, wide_place[NB + p], place_lat)
    cells = jnp.where(lateral, place_lat * BLOCK + by_block % BLOCK, by_block)

    tracer_rim = exchange(first_sends(tracer_ratio, wide_list, order, WR))
    table = tracer_table(tracer_ratio, tracer_rim)
    parts = [
        edge_tracer_part(table, cells[:, i : i + T_STEP].reshape(-1), i)
        for i in range(0, NE + LAT + 2 * ER, T_STEP)
    ]
    edge_tracer = jnp.concatenate(parts, axis=0)

    g_info = (g_pattern, cell_place, edge_list, order)
    d_info = (d_pattern, edge_place, cell_list, order)
    mass, wind = mass_field, normal_wind
    winds, rims = [], []
    for substep in range(SUBSTEPS):
        if substep > 0:
            rim = exchange(sends)
        wind, sends = gradient(g_info, mass, wind, g_weights, rim)
        rim = exchange(sends)
        winds.append(wind)
        rims.append(rim)
        mass, sends = divergence(d_info, wind, mass, d_weights, vertical_inverse, rim)
    total = functools.reduce(jnp.add, winds)
    total_rim = [functools.reduce(jnp.add, parts) for parts in zip(*rims)]
    tracer_final = transport(d_pattern, edge_place, total, tracer_ratio, d_weights, edge_tracer, total_rim)
    return mass, wind, tracer_final


def solution(mesh):
    both = ("region", "sub")
    return jax.shard_map(
        body,
        mesh=mesh,
        in_specs=(
            P(None, both),
            P(None, both),
            P(None, both),
            P(both, None, None, None),
            P(both, None, None, None),
            P(both, None, None),
            P(both, None),
            P(both, None),
            P(None, both),
            P(both, None),
            P(both, None),
            P(both, None),
        ),
        out_specs=(P(None, both), P(None, both), P(None, both)),
        check_vma=False,
    )
```

```python
import functools

import numpy as np
import jax
import jax.numpy as jnp
from jax import lax
from jax.experimental import pallas as pl
from jax.experimental.pallas import tpu as pltpu
from jax.sharding import PartitionSpec as P

BLOCK = 128
LEV = 96
NB = 24
NE = 36
KG = 3
KD = 4
SR = 4
ER = 4
WR = 8
SUBSTEPS = 5
N_REGION = 16
N_CHIP = 4
N_SUB = 8
LAT = 8

time_step = 0.25
tracer_step = 0.5

BF = jnp.bfloat16
F32 = jnp.float32

ALONG = [(2 * x + c, 2 * ((x + (1 if c == 0 else 3)) % 4) + c) for x in range(4) for c in range(2)]
ACROSS = [(2 * x + c, 2 * ((x + 2) % 4) + c) for x in range(4) for c in range(2)]
MATES = [(s, s ^ 1) for s in range(8)]
REGIONS = [(r * 8 + s, (r + (1 if s % 2 == 0 else 15)) % 16 * 8 + s) for r in range(16) for s in range(8)]


def send_order(side):
    rows = []
    for s in range(N_SUB):
        x, c = divmod(s, 2)
        mine = (x + (1 if c == 0 else 3)) % 4
        other = (x + (3 if c == 0 else 1)) % 4
        far = (x + 2) % 4
        o = 1 - c
        to_next = [LAT + j for j in range(side)]
        to_prev = [LAT + side + j for j in range(side)]
        kept, given = (to_next, to_prev) if c == 0 else (to_prev, to_next)
        rows.append(
            [2 * x + o, 2 * other + o, 2 * other + c, *given]
            + [2 * mine + c, 2 * mine + o, 2 * far + c, 2 * far + o, *kept]
        )
    return np.array(rows, np.int32)


def lateral_place():
    rows = []
    for s in range(N_SUB):
        x, c = divmod(s, 2)
        back = 3 if c == 0 else 1
        row = []
        for p in range(N_SUB):
            px, pc = divmod(p, 2)
            d = (px - x) % 4
            same = pc == c
            if d == 0:
                row.append(7 if same else 0)
            elif d == back:
                row.append(1 if same else 2)
            elif d == 2:
                row.append(3 if same else 6)
            else:
                row.append(5 if same else 4)
        rows.append(row)
    return np.array(rows, np.int32)


def place_table(own, side):
    lat = lateral_place()
    rows = []
    for s in range(N_SUB):
        first, second = np.arange(side), side + np.arange(side)
        prev, nxt = (first, second) if s % 2 == 0 else (second, first)
        rows.append(np.concatenate([np.arange(own), own + lat[s], own + LAT + prev, own + LAT + nxt]))
    return np.stack(rows).astype(np.int32)


def row_of(table):
    sub = lax.axis_index("sub")
    return lax.dynamic_slice(jnp.asarray(table), (sub, 0), (1, table.shape[1]))[0]


def exchange(sends, work, *given):
    pre, along, across, region = sends
    pre_in = lax.ppermute(pre, "sub", MATES)
    pre_in, *given = together(pre_in, *given)
    region_in = lax.ppermute(jnp.concatenate([region, pre_in[3:]], axis=0), ("region", "sub"), REGIONS)
    along_in = lax.ppermute(jnp.concatenate([along, pre_in[1:3]], axis=0), "sub", ALONG)
    across_in = lax.ppermute(across, "sub", ACROSS)
    side = region.shape[0]
    done, along_in, across_in, region_in = together(work(*given), along_in, across_in, region_in)
    post = jnp.concatenate([along_in[1:2], along_in[3:4], across_in[1:2], region_in[side:]], axis=0)
    post_in = lax.ppermute(post, "sub", MATES)
    return done, (pre_in, along_in, across_in, region_in, post_in)


def two_parts(x):
    hi = x.astype(BF)
    lo = (x - hi.astype(F32)).astype(BF)
    return hi, lo


VMEM = pl.BlockSpec(memory_space=pltpu.VMEM)
SMEM = pl.BlockSpec(memory_space=pltpu.SMEM)
HBM = pl.BlockSpec(memory_space=pltpu.HBM)
PARAMS = pltpu.CompilerParams(vmem_limit_bytes=16 << 20)
BIG = pltpu.CompilerParams(vmem_limit_bytes=40 << 20)
BIGGEST = pltpu.CompilerParams(vmem_limit_bytes=58 << 20)


def cost(flops, moved):
    return pl.CostEstimate(flops=flops, bytes_accessed=moved, transcendentals=0)


GROUP = 6
CUT = 12
READS = 6
G_TERMS = NE * KG
D_TERMS = NB * KD
G_RIM = NE * (KG - 1) + GROUP
D_RIM = D_TERMS + GROUP
G_AT = G_TERMS + D_TERMS
D_AT = G_AT + G_RIM
ALL_TERMS = D_AT + D_RIM


def split_kernel(g_pattern, d_pattern, g_ref, d_ref, out_ref, raw, cut, rim, in_sem, out_sem, rim_sem):
    g_steps, d_steps = G_TERMS // CUT, D_TERMS // CUT
    steps = g_steps + d_steps

    def read(i):
        ref, j = (g_ref, i) if i < g_steps else (d_ref, i - g_steps)
        return pltpu.make_async_copy(ref.at[pl.ds(j * CUT, CUT)], raw.at[i % READS], in_sem.at[i])

    def write(i):
        return pltpu.make_async_copy(cut.at[i], out_ref.at[pl.ds(i * CUT, CUT)], out_sem.at[i])

    def write_rim(at, g):
        rows = pl.ds(at + g * GROUP, GROUP)
        return pltpu.make_async_copy(rim.at[rows], out_ref.at[pl.ds(at + G_AT + g * GROUP, GROUP)], rim_sem.at[at // GROUP + g])

    def finish(at, n):
        for j in range(GROUP):
            rim[n + j] = jnp.zeros((BLOCK, 2 * BLOCK), BF)
        groups = (n - at + GROUP - 1) // GROUP

        def one(g, _):
            write_rim(at, g).start()
            return 0

        lax.fori_loop(0, groups, one, 0)
        return groups

    for i in range(READS):
        read(i).start()
    n = jnp.int32(0)
    for i in range(steps):
        read(i).wait()
        pattern, own, start = (g_pattern, NB, i * CUT) if i < g_steps else (d_pattern, NE, (i - g_steps) * CUT)
        if i == g_steps:
            g_groups = finish(0, n)
            n = jnp.int32(G_RIM)

        def one(j, n):
            hi, lo = two_parts(raw[i % READS, j])
            both = jnp.concatenate([hi, lo], axis=1)
            cut[i, j] = both
            rim[n] = both
            return n + (pattern[start + j] >= own).astype(jnp.int32)

        n = lax.fori_loop(0, CUT, one, n, unroll=4)
        write(i).start()
        if i + READS < steps:
            read(i + READS).start()
    d_groups = finish(G_RIM, n)
    for i in range(steps):
        write(i).wait()
    for at, groups in ((0, g_groups), (G_RIM, d_groups)):

        def done(g, _, at=at):
            write_rim(at, g).wait()
            return 0

        lax.fori_loop(0, groups, done, 0)


def split_weights(g_pattern, d_pattern, g, d):
    steps = (G_TERMS + D_TERMS) // CUT
    return pl.pallas_call(
        split_kernel,
        in_specs=[SMEM, SMEM, HBM, HBM],
        out_specs=HBM,
        out_shape=jax.ShapeDtypeStruct((ALL_TERMS, BLOCK, 2 * BLOCK), BF),
        scratch_shapes=[
            pltpu.VMEM((READS, CUT, BLOCK, BLOCK), F32),
            pltpu.VMEM((steps, CUT, BLOCK, 2 * BLOCK), BF),
            pltpu.VMEM((G_RIM + D_RIM, BLOCK, 2 * BLOCK), BF),
            pltpu.SemaphoreType.DMA((steps,)),
            pltpu.SemaphoreType.DMA((steps,)),
            pltpu.SemaphoreType.DMA(((G_RIM + D_RIM) // GROUP,)),
        ],
        compiler_params=BIGGEST,
        cost_estimate=cost(0, 30 << 20),
        name="split_weights",
    )(g_pattern, d_pattern, g.reshape(-1, BLOCK, BLOCK), d.reshape(-1, BLOCK, BLOCK))


def split_inverse_kernel(v_ref, o_ref):
    hi, lo = two_parts(v_ref[...])
    o_ref[:, :LEV] = hi
    o_ref[:, LEV:] = lo


def split_inverse(inverse):
    return pl.pallas_call(
        split_inverse_kernel,
        grid=(4,),
        in_specs=[pl.BlockSpec((NB // 4, LEV, LEV), lambda i: (i, 0, 0))],
        out_specs=pl.BlockSpec((NB // 4, 2 * LEV, LEV), lambda i: (i, 0, 0)),
        out_shape=jax.ShapeDtypeStruct((NB, 2 * LEV, LEV), BF),
        compiler_params=PARAMS,
        cost_estimate=cost(NB * LEV * LEV * 4, NB * LEV * LEV * 8),
        name="split_inverse",
    )(inverse)


ROOM = 128


def list_kernel(pattern, place, slot, target, count, *, own, targets, width):
    def one(t, n):
        for k in range(width):
            e = pattern[t * width + k]
            slot[n] = place[e] - own
            target[n] = t
            n = n + (e >= own).astype(jnp.int32)
        return n

    n = lax.fori_loop(0, targets, one, jnp.int32(0))
    for j in range(GROUP):
        slot[n + j] = LAT - 1
        target[n + j] = 0
    count[0] = (n + GROUP - 1) // GROUP


def rim_list(pattern, place, own, targets, width):
    room = jax.ShapeDtypeStruct((ROOM,), jnp.int32)
    return pl.pallas_call(
        functools.partial(list_kernel, own=own, targets=targets, width=width),
        in_specs=[SMEM] * 2,
        out_specs=[SMEM] * 3,
        out_shape=[room] * 2 + [jax.ShapeDtypeStruct((1,), jnp.int32)],
        compiler_params=PARAMS,
        name="rim_list",
    )(pattern, place)


RIM = ((0, 0), (1, 0), (1, 2), (2, 0), (4, 0), (4, 1), (4, 2))


def rim_blocks(rim, side):
    blocks = [(j, rim[which], i) for j, (which, i) in enumerate(RIM)]
    blocks += [(LAT + i, rim[3], i) for i in range(side)]
    blocks += [(LAT + side + i, rim[4], 3 + i) for i in range(side)]
    return blocks


def store_parts(ext, slot, x):
    hi, lo = two_parts(x)
    ext[slot, :LEV, :] = hi
    ext[slot, LEV:, :] = lo


def columns(b):
    return pl.ds(b * BLOCK if isinstance(b, int) else pl.multiple_of(b * BLOCK, BLOCK), BLOCK)


def block_at(ref, b):
    return ref[:, columns(b)]


def summed(y):
    return (y[:LEV, :BLOCK] + y[LEV:, :BLOCK]) + (y[:LEV, BLOCK:] + y[LEV:, BLOCK:])


def pick(source, entry):
    live = (entry >= 0).astype(F32)
    return source(jnp.maximum(entry, 0)) * live


def fill_sends(sends, send_list, order, source, side):
    at = 0
    for ref, n in zip(sends, (3 + side, 2, 2, side)):
        for j in range(n):
            ref[j] = pick(source, send_list[order[at + j]])
        at += n


def send_shapes(side):
    return [jax.ShapeDtypeStruct((n, LEV, BLOCK), F32) for n in (3 + side, 2, 2, side)]


def first_kernel(send_list, order, field_ref, *sends, side):
    fill_sends(sends, send_list, order, lambda b: block_at(field_ref, b), side)


def first_sends(field, send_list, order, side):
    return pl.pallas_call(
        functools.partial(first_kernel, side=side),
        in_specs=[SMEM, SMEM, VMEM],
        out_specs=[VMEM] * 4,
        out_shape=send_shapes(side),
        compiler_params=PARAMS,
        name="first_sends",
    )(send_list, order, field)


UNROLL = 6
SOLVED = 8


def own_kernel(pattern, *refs, own, targets, width, first, scale, flux):
    if flux:
        source_ref, edge_ref, start_ref, w_ref, out_ref, ext, wbuf, sems = refs
    else:
        source_ref, start_ref, w_ref, out_ref, ext, wbuf, sems = refs
    groups, size = targets // UNROLL, UNROLL * width

    def fetch(i):
        return pltpu.make_async_copy(w_ref.at[pl.ds(first + i * size, size)], wbuf.at[i], sems.at[i])

    for i in range(groups):
        fetch(i).start()

    def fill(b, _):
        x = block_at(source_ref, b)
        if flux:
            x = (x / SUBSTEPS) * edge_ref[b]
        store_parts(ext, b, x)
        return 0

    lax.fori_loop(0, own, fill, 0, unroll=4)
    ext[own] = jnp.zeros((2 * LEV, BLOCK), BF)

    def some(i, _):
        fetch(i).wait()
        for j in range(UNROLL):
            t = i * UNROLL + j
            x = jnp.concatenate([ext[jnp.minimum(pattern[t * width + k], own)] for k in range(width)], axis=1)
            w = wbuf[i, j * width : (j + 1) * width].reshape(width * BLOCK, 2 * BLOCK)
            y = jnp.dot(x, w, preferred_element_type=F32)
            out_ref[:, columns(t)] = block_at(start_ref, t) - scale * summed(y)
        return 0

    lax.fori_loop(0, groups, some, 0)


def own_product(pattern, source, start, weights, own, targets, width, first, scale, edge=None):
    ins = [source] + ([] if edge is None else [edge]) + [start, weights]
    return pl.pallas_call(
        functools.partial(own_kernel, own=own, targets=targets, width=width, first=first, scale=scale, flux=edge is not None),
        in_specs=[SMEM] + [VMEM] * (len(ins) - 1) + [HBM],
        out_specs=VMEM,
        out_shape=jax.ShapeDtypeStruct(start.shape, F32),
        scratch_shapes=[
            pltpu.VMEM((own + 1, 2 * LEV, BLOCK), BF),
            pltpu.VMEM((targets // UNROLL, UNROLL * width, BLOCK, 2 * BLOCK), BF),
            pltpu.SemaphoreType.DMA((targets // UNROLL,)),
        ],
        compiler_params=BIG,
        cost_estimate=cost(4 << 30, 8 << 20),
        name="own_product",
    )(pattern, *ins)


def rim_kernel(slot, target, count, *refs, targets, side, next_side, first, scale, flux, solve):
    refs = list(refs)
    held = refs.pop(0) if flux else None
    if next_side:
        send_list, order = refs.pop(0), refs.pop(0)
    partial_ref, w_ref = refs.pop(0), refs.pop(0)
    rim, refs = refs[:5], refs[5:]
    edge_ref = refs.pop(0) if flux else None
    inv_ref = refs.pop(0) if solve else None
    out_ref = refs.pop(0)
    sends, refs = (refs[:4], refs[4:]) if next_side else ((), refs)
    ext, wbuf, sems = refs.pop(0), refs.pop(0), refs.pop(0)
    acc = refs.pop(0) if solve else out_ref

    def fetch(g):
        return pltpu.make_async_copy(w_ref.at[pl.ds(first + g * GROUP, GROUP)], wbuf.at[pl.ds(g * GROUP, GROUP)], sems.at[g])

    def begin(g, _):
        fetch(g).start()
        return 0

    lax.fori_loop(0, count[0], begin, 0)
    for j, ref, i in rim_blocks(rim, side):
        x = ref[i]
        if flux:
            x = (x / SUBSTEPS) * edge_ref[held[NE + j]]
        store_parts(ext, j, x)
    ext[LAT - 1] = jnp.zeros((2 * LEV, BLOCK), BF)
    acc[...] = partial_ref[...]

    def some(i, _):
        at = i * GROUP
        parts = []
        fetch(i).wait()
        for j in range(GROUP):
            y = jnp.dot(ext[slot[at + j]], wbuf[at + j], preferred_element_type=F32)
            parts.append(scale * summed(y))
        for j in range(GROUP):
            t = target[at + j]
            acc[:, columns(t)] = block_at(acc, t) - parts[j]
        return 0

    lax.fori_loop(0, count[0], some, 0)

    if solve:
        def solved(i, _):
            for j in range(SOLVED):
                b = i * SOLVED + j
                p_hi, p_lo = two_parts(block_at(acc, b))
                y = jnp.dot(inv_ref[b], jnp.concatenate([p_hi, p_lo], axis=1), preferred_element_type=F32)
                out_ref[:, columns(b)] = summed(y)
            return 0

        lax.fori_loop(0, targets // SOLVED, solved, 0)
    if next_side:
        fill_sends(sends, send_list, order, lambda b: block_at(out_ref, b), next_side)


def rim_product(lists, partial, weights, rim, targets, side, scale, sends=None, next_side=0, edge=None, held=None, inverse=None):
    ins = [partial, weights, *rim]
    if edge is not None:
        ins.append(edge)
    if inverse is not None:
        ins.append(inverse)
    scalars = [*lists] + ([] if edge is None else [held]) + ([] if sends is None else [*sends])
    out_shape = [jax.ShapeDtypeStruct(partial.shape, F32)] + (send_shapes(next_side) if next_side else [])
    rim_terms = G_RIM if targets == NE else D_RIM
    scratch = [
        pltpu.VMEM((LAT + 2 * side, 2 * LEV, BLOCK), BF),
        pltpu.VMEM((rim_terms, BLOCK, 2 * BLOCK), BF),
        pltpu.SemaphoreType.DMA((rim_terms // GROUP,)),
    ]
    if inverse is not None:
        scratch.append(pltpu.VMEM(partial.shape, F32))
    out = pl.pallas_call(
        functools.partial(
            rim_kernel, targets=targets, side=side, next_side=next_side, first=G_AT if targets == NE else D_AT, scale=scale, flux=edge is not None, solve=inverse is not None
        ),
        in_specs=[SMEM] * len(scalars) + [VMEM, HBM] + [VMEM] * (len(ins) - 2),
        out_specs=[VMEM] * len(out_shape),
        out_shape=out_shape,
        scratch_shapes=scratch,
        compiler_params=BIG,
        cost_estimate=cost(1 << 30, 4 << 20),
        name="rim_product",
    )(*scalars, *ins)
    return out[0], out[1:]


ROWS_AT_ONCE = 32
PARTS = (8, 8, 8, 8, 8, 8, 4)


def turned(x):
    return jnp.transpose(x, (1, 0))


def table_kernel(held, tracer_ref, *refs):
    rim, table_ref = refs[:5], refs[5]

    def put(slot, x):
        padded = jnp.concatenate([x, jnp.zeros((BLOCK - LEV, BLOCK), F32)], axis=0)
        table_ref[columns(slot), :] = turned(padded)

    def one(b, _):
        put(b, block_at(tracer_ref, b))
        return 0

    lax.fori_loop(0, NB, one, 0, unroll=2)
    for j, ref, i in rim_blocks(rim, WR):
        put(held[NB + j], ref[i])
    put(held[NB + LAT - 1], jnp.zeros((LEV, BLOCK), F32))


def tracer_table(held, tracer, rim):
    cells = (NB + LAT + 2 * WR) * BLOCK
    return pl.pallas_call(
        table_kernel,
        in_specs=[SMEM] + [VMEM] * 6,
        out_specs=VMEM,
        out_shape=jax.ShapeDtypeStruct((cells, BLOCK), F32),
        compiler_params=PARAMS,
        cost_estimate=cost(0, 8 << 20),
        name="tracer_table",
    )(held, tracer, *rim)


def edge_tracer_kernel(cells_ref, table_ref, out_ref, rows, cells, sem, *, start, blocks):
    fetch = pltpu.make_async_copy(cells_ref.at[:, pl.ds(start * BLOCK, blocks * BLOCK)], cells, sem)
    fetch.start()
    fetch.wait()

    def block(e, _):
        def some(i, _):
            at = e * BLOCK + i * ROWS_AT_ONCE
            sums = []
            for j in range(ROWS_AT_ONCE):
                a = table_ref[pl.ds(cells[0, at + j], 1), :]
                b = table_ref[pl.ds(cells[1, at + j], 1), :]
                sums.append(a + b)
            for j in range(ROWS_AT_ONCE):
                rows[pl.ds(i * ROWS_AT_ONCE + j, 1), :] = sums[j]
            return 0

        lax.fori_loop(0, BLOCK // ROWS_AT_ONCE, some, 0)
        out_ref[e] = 0.5 * turned(rows[...])[:LEV]
        return 0

    lax.fori_loop(0, blocks, block, 0)


def edge_tracer_part(table, cells, start, blocks):
    return pl.pallas_call(
        functools.partial(edge_tracer_kernel, start=start, blocks=blocks),
        in_specs=[HBM, VMEM],
        out_specs=VMEM,
        out_shape=jax.ShapeDtypeStruct((blocks, LEV, BLOCK), F32),
        scratch_shapes=[
            pltpu.VMEM((BLOCK, BLOCK), F32),
            pltpu.SMEM((2, blocks * BLOCK), jnp.int32),
            pltpu.SemaphoreType.DMA,
        ],
        compiler_params=PARAMS,
        cost_estimate=cost(0, 8 << 20),
        name="edge_tracer",
    )(cells, table)


def held_table(own, side):
    return np.argsort(place_table(own, side), axis=1).astype(np.int32)


def together(*xs):
    return lax.optimization_barrier(xs)


def body(
    mass_field,
    normal_wind,
    tracer_ratio,
    gradient_weights,
    divergence_weights,
    vertical_inverse,
    gradient_pattern,
    divergence_pattern,
    edge_cells,
    cell_sends,
    edge_sends,
    wide_sends,
):
    order = row_of(send_order(SR))
    wide_order = row_of(send_order(WR))
    cell_place = row_of(place_table(NB, SR))
    edge_place = row_of(place_table(NE, ER))
    cell_list, edge_list, wide_list = cell_sends[0], edge_sends[0], wide_sends[0]
    g_pattern = gradient_pattern.reshape(-1)
    d_pattern = divergence_pattern.reshape(-1)

    wide_held = row_of(held_table(NB, WR))
    edge_held = row_of(held_table(NE, ER))

    def g_own(mass, wind):
        return own_product(g_pattern, mass, wind, weights, NB, NE, KG, 0, time_step)

    def d_own(source, start, scale, edge=None):
        return own_product(d_pattern, source, start, weights, NE, NB, KD, G_TERMS, scale, edge)

    def prepared():
        nonlocal weights
        weights = split_weights(g_pattern, d_pattern, gradient_weights, divergence_weights)
        v = split_inverse(vertical_inverse)
        g_terms = rim_list(g_pattern, cell_place, NB, NE, KG)
        d_terms = rim_list(d_pattern, edge_place, NE, NB, KD)
        return together(g_own(mass_field, normal_wind), v, *g_terms, *d_terms)

    weights = None
    first = first_sends(mass_field, cell_list, order, SR)
    wide = first_sends(tracer_ratio, wide_list, wide_order, WR)
    done, rim = exchange(first, prepared)
    partial, inverse, g_terms, d_terms = done[0], done[1], done[2:5], done[5:]
    tracer_rim = exchange(wide, lambda: ())[1]
    edge_parts = []
    table = None

    def tracer_work(window, partial):
        nonlocal table
        if window == 1:
            partial, *rim = together(partial, *tracer_rim)
            table = tracer_table(wide_held, tracer_ratio, rim)
            partial, table = together(partial, table)
        elif window - 2 < len(PARTS):
            blocks, start = PARTS[window - 2], sum(PARTS[: window - 2])
            partial, now = together(partial, table)
            part = edge_tracer_part(now, edge_cells, start, blocks)
            partial, part = together(partial, part)
            edge_parts.append(part)
        return partial

    mass, wind = mass_field, normal_wind
    winds, rims = [], []
    for substep in range(SUBSTEPS):
        if substep > 0:
            partial, rim = exchange(sends, lambda m, w: tracer_work(2 * substep, g_own(m, w)), mass, wind)
        wind, sends = rim_product(g_terms, partial, weights, rim, NE, SR, time_step, (edge_list, order), ER)
        winds.append(wind)
        if substep < SUBSTEPS - 1:
            partial, rim = exchange(sends, lambda w, m: tracer_work(2 * substep + 1, d_own(w, m, time_step)), wind, mass)
        else:

            def last_work(w, m, *earlier):
                edge_tracer = jnp.concatenate(edge_parts, axis=0)
                total = functools.reduce(jnp.add, (*earlier, w))
                partial, total, tracer = together(d_own(w, m, time_step), total, tracer_ratio)
                return partial, d_own(total, tracer, tracer_step, edge_tracer), edge_tracer

            (partial, t_partial, edge_tracer), rim = exchange(sends, last_work, wind, mass, *winds[:-1])
        rims.append(rim)
        if substep < SUBSTEPS - 1:
            mass, sends = rim_product(d_terms, partial, weights, rim, NB, ER, time_step, (cell_list, order), SR, inverse=inverse)
        else:
            mass, _ = rim_product(d_terms, partial, weights, rim, NB, ER, time_step, inverse=inverse)
    total_rim = [functools.reduce(jnp.add, parts) for parts in zip(*rims)]
    tracer_final, _ = rim_product(d_terms, t_partial, weights, total_rim, NB, ER, tracer_step, edge=edge_tracer, held=edge_held)
    return mass, wind, tracer_final


def solution(mesh):
    both = ("region", "sub")
    return jax.shard_map(
        body,
        mesh=mesh,
        in_specs=(
            P(None, both),
            P(None, both),
            P(None, both),
            P(both, None, None, None),
            P(both, None, None, None),
            P(both, None, None),
            P(both, None),
            P(both, None),
            P(None, both),
            P(both, None),
            P(both, None),
            P(both, None),
        ),
        out_specs=(P(None, both), P(None, both), P(None, both)),
        check_vma=False,
    )
```

```python
import functools

import numpy as np
import jax
import jax.numpy as jnp
from jax import lax
from jax.experimental import pallas as pl
from jax.experimental.pallas import tpu as pltpu
from jax.sharding import PartitionSpec as P

BLOCK = 128
LEV = 96
NB = 24
NE = 36
KG = 3
KD = 4
SR = 4
ER = 4
WR = 8
SUBSTEPS = 5
N_REGION = 16
N_CHIP = 4
N_SUB = 8
LAT = 8

time_step = 0.25
tracer_step = 0.5

BF = jnp.bfloat16
F32 = jnp.float32

ALONG = [(2 * x + c, 2 * ((x + (1 if c == 0 else 3)) % 4) + c) for x in range(4) for c in range(2)]
ACROSS = [(2 * x + c, 2 * ((x + 2) % 4) + c) for x in range(4) for c in range(2)]
MATES = [(s, s ^ 1) for s in range(8)]
REGIONS = [(r * 8 + s, (r + (1 if s % 2 == 0 else 15)) % 16 * 8 + s) for r in range(16) for s in range(8)]


def send_order(side):
    rows = []
    for s in range(N_SUB):
        x, c = divmod(s, 2)
        mine = (x + (1 if c == 0 else 3)) % 4
        other = (x + (3 if c == 0 else 1)) % 4
        far = (x + 2) % 4
        o = 1 - c
        to_next = [LAT + j for j in range(side)]
        to_prev = [LAT + side + j for j in range(side)]
        kept, given = (to_next, to_prev) if c == 0 else (to_prev, to_next)
        rows.append(
            [2 * x + o, 2 * other + o, 2 * other + c, *given]
            + [2 * mine + c, 2 * mine + o, 2 * far + c, 2 * far + o, *kept]
        )
    return np.array(rows, np.int32)


def lateral_place():
    rows = []
    for s in range(N_SUB):
        x, c = divmod(s, 2)
        back = 3 if c == 0 else 1
        row = []
        for p in range(N_SUB):
            px, pc = divmod(p, 2)
            d = (px - x) % 4
            same = pc == c
            if d == 0:
                row.append(7 if same else 0)
            elif d == back:
                row.append(1 if same else 2)
            elif d == 2:
                row.append(3 if same else 6)
            else:
                row.append(5 if same else 4)
        rows.append(row)
    return np.array(rows, np.int32)


def place_table(own, side):
    lat = lateral_place()
    rows = []
    for s in range(N_SUB):
        first, second = np.arange(side), side + np.arange(side)
        prev, nxt = (first, second) if s % 2 == 0 else (second, first)
        rows.append(np.concatenate([np.arange(own), own + lat[s], own + LAT + prev, own + LAT + nxt]))
    return np.stack(rows).astype(np.int32)


def held_table(own, side):
    return np.argsort(place_table(own, side), axis=1).astype(np.int32)


class At:
    def __init__(self, ref, start):
        self.ref, self.start = ref, start

    def __getitem__(self, i):
        return self.ref[self.start + i]


def all_tables():
    tables = dict(
        order=send_order(SR),
        wide_order=send_order(WR),
        cell_place=place_table(NB, SR),
        edge_place=place_table(NE, ER),
        wide_held=held_table(NB, WR),
        edge_held=held_table(NE, ER),
    )
    starts, at = {}, 0
    for name, table in tables.items():
        starts[name] = at
        at += table.shape[1]
    return np.concatenate(list(tables.values()), axis=1), starts


TABLES, STARTS = all_tables()


def row_of_tables():
    sub = lax.axis_index("sub")
    return lax.dynamic_slice(jnp.asarray(TABLES), (sub, 0), (1, TABLES.shape[1]))[0]


def hand_over(sends):
    return lax.ppermute(sends[0], "sub", MATES)


def exchange(sends, work, *given):
    pre_in, *given = together(hand_over(sends), *given)
    return travel(sends, pre_in, work, *given)


def travel(sends, pre_in, work, *given):
    _, along, across, region = sends
    region_in = lax.ppermute(jnp.concatenate([region, pre_in[3:]], axis=0), ("region", "sub"), REGIONS)
    along_in = lax.ppermute(jnp.concatenate([along, pre_in[1:3]], axis=0), "sub", ALONG)
    across_in = lax.ppermute(across, "sub", ACROSS)
    side = region.shape[0]
    done, along_in, across_in, region_in = together(work(*given), along_in, across_in, region_in)
    post = jnp.concatenate([along_in[1:2], along_in[3:4], across_in[1:2], region_in[side:]], axis=0)
    post_in = lax.ppermute(post, "sub", MATES)
    return done, (pre_in, along_in, across_in, region_in, post_in)


def two_parts(x):
    hi = x.astype(BF)
    lo = (x - hi.astype(F32)).astype(BF)
    return hi, lo


VMEM = pl.BlockSpec(memory_space=pltpu.VMEM)
SMEM = pl.BlockSpec(memory_space=pltpu.SMEM)
HBM = pl.BlockSpec(memory_space=pltpu.HBM)
PARAMS = pltpu.CompilerParams(vmem_limit_bytes=16 << 20)
BIG = pltpu.CompilerParams(vmem_limit_bytes=40 << 20)
BIGGEST = pltpu.CompilerParams(vmem_limit_bytes=58 << 20)


def cost(flops, moved):
    return pl.CostEstimate(flops=flops, bytes_accessed=moved, transcendentals=0)


GROUP = 6
ROOM = 128
CUT = 12
READS = 6
G_TERMS = NE * KG
D_TERMS = NB * KD
G_RIM = NE * (KG - 1) + GROUP
D_RIM = D_TERMS + GROUP
G_AT = G_TERMS + D_TERMS
D_AT = G_AT + G_RIM
ALL_TERMS = D_AT + D_RIM


def split_kernel(g_pattern, d_pattern, info, g_ref, d_ref, out_ref, g_slot, g_target, g_count, d_slot, d_target, d_count, raw, cut, rim, in_sem, out_sem, rim_sem):
    g_steps, d_steps = G_TERMS // CUT, D_TERMS // CUT
    steps = g_steps + d_steps

    def read(i):
        ref, j = (g_ref, i) if i < g_steps else (d_ref, i - g_steps)
        return pltpu.make_async_copy(ref.at[pl.ds(j * CUT, CUT)], raw.at[i % READS], in_sem.at[i])

    def write(i):
        return pltpu.make_async_copy(cut.at[i], out_ref.at[pl.ds(i * CUT, CUT)], out_sem.at[i])

    def write_rim(at, g):
        rows = pl.ds(at + g * GROUP, GROUP)
        return pltpu.make_async_copy(rim.at[rows], out_ref.at[pl.ds(at + G_AT + g * GROUP, GROUP)], rim_sem.at[at // GROUP + g])

    def finish(at, n, slot, target, count):
        for j in range(GROUP):
            rim[n + j] = jnp.zeros((BLOCK, 2 * BLOCK), BF)
            slot[n - at + j] = LAT - 1
            target[n - at + j] = 0
        groups = (n - at + GROUP - 1) // GROUP
        count[0] = groups

        def one(g, _):
            write_rim(at, g).start()
            return 0

        lax.fori_loop(0, groups, one, 0)
        return groups

    for i in range(READS):
        read(i).start()
    n = jnp.int32(0)
    for i in range(steps):
        read(i).wait()
        if i < g_steps:
            pattern, own, start, at, width, lists = g_pattern, NB, i * CUT, 0, KG, (g_slot, g_target)
            place = At(info, STARTS["cell_place"])
        else:
            pattern, own, start, at, width, lists = d_pattern, NE, (i - g_steps) * CUT, G_RIM, KD, (d_slot, d_target)
            place = At(info, STARTS["edge_place"])
        if i == g_steps:
            g_groups = finish(0, n, g_slot, g_target, g_count)
            n = jnp.int32(G_RIM)

        def one(j, n):
            hi, lo = two_parts(raw[i % READS, j])
            both = jnp.concatenate([hi, lo], axis=1)
            cut[i, j] = both
            rim[n] = both
            e = pattern[start + j]
            slot, target = lists
            slot[n - at] = place[e] - own
            target[n - at] = start // width + (j * 43 >> 7 if width == 3 else j >> 2)
            return n + (e >= own).astype(jnp.int32)

        n = lax.fori_loop(0, CUT, one, n, unroll=4)
        write(i).start()
        if i + READS < steps:
            read(i + READS).start()
    d_groups = finish(G_RIM, n, d_slot, d_target, d_count)
    for i in range(steps):
        write(i).wait()
    for at, groups in ((0, g_groups), (G_RIM, d_groups)):

        def done(g, _, at=at):
            write_rim(at, g).wait()
            return 0

        lax.fori_loop(0, groups, done, 0)


def split_weights(g_pattern, d_pattern, info, g, d):
    steps = (G_TERMS + D_TERMS) // CUT
    return pl.pallas_call(
        split_kernel,
        in_specs=[SMEM] * 3 + [HBM] * 2,
        out_specs=[HBM] + [SMEM] * 6,
        out_shape=[jax.ShapeDtypeStruct((ALL_TERMS, BLOCK, 2 * BLOCK), BF)]
        + [jax.ShapeDtypeStruct((n,), jnp.int32) for n in (ROOM, ROOM, 1)] * 2,
        scratch_shapes=[
            pltpu.VMEM((READS, CUT, BLOCK, BLOCK), F32),
            pltpu.VMEM((steps, CUT, BLOCK, 2 * BLOCK), BF),
            pltpu.VMEM((G_RIM + D_RIM, BLOCK, 2 * BLOCK), BF),
            pltpu.SemaphoreType.DMA((steps,)),
            pltpu.SemaphoreType.DMA((steps,)),
            pltpu.SemaphoreType.DMA(((G_RIM + D_RIM) // GROUP,)),
        ],
        compiler_params=BIGGEST,
        cost_estimate=cost(0, 30 << 20),
        name="split_weights",
    )(g_pattern, d_pattern, info, g.reshape(-1, BLOCK, BLOCK), d.reshape(-1, BLOCK, BLOCK))


def split_inverse_kernel(v_ref, o_ref):
    hi, lo = two_parts(v_ref[...])
    o_ref[:, :LEV] = hi
    o_ref[:, LEV:] = lo


def split_inverse(inverse):
    return pl.pallas_call(
        split_inverse_kernel,
        grid=(4,),
        in_specs=[pl.BlockSpec((NB // 4, LEV, LEV), lambda i: (i, 0, 0))],
        out_specs=pl.BlockSpec((NB // 4, 2 * LEV, LEV), lambda i: (i, 0, 0)),
        out_shape=jax.ShapeDtypeStruct((NB, 2 * LEV, LEV), BF),
        compiler_params=PARAMS,
        cost_estimate=cost(NB * LEV * LEV * 4, NB * LEV * LEV * 8),
        name="split_inverse",
    )(inverse)


RIM = ((0, 0), (1, 0), (1, 2), (2, 0), (4, 0), (4, 1), (4, 2))


def rim_blocks(rim, side):
    blocks = [(j, rim[which], i) for j, (which, i) in enumerate(RIM)]
    blocks += [(LAT + i, rim[3], i) for i in range(side)]
    blocks += [(LAT + side + i, rim[4], 3 + i) for i in range(side)]
    return blocks


def store_parts(ext, slot, x):
    hi, lo = two_parts(x)
    ext[slot, :LEV, :] = hi
    ext[slot, LEV:, :] = lo


def columns(b):
    return pl.ds(b * BLOCK if isinstance(b, int) else pl.multiple_of(b * BLOCK, BLOCK), BLOCK)


def block_at(ref, b):
    return ref[:, columns(b)]


def summed(y):
    return (y[:LEV, :BLOCK] + y[LEV:, :BLOCK]) + (y[:LEV, BLOCK:] + y[LEV:, BLOCK:])


def pick(source, entry):
    live = (entry >= 0).astype(F32)
    return source(jnp.maximum(entry, 0)) * live


def fill_sends(sends, send_list, info, source, side):
    order = At(info, STARTS["order" if side == SR else "wide_order"])
    at = 0
    for ref, n in zip(sends, (3 + side, 2, 2, side)):
        for j in range(n):
            ref[j] = pick(source, send_list[order[at + j]])
        at += n


def send_shapes(side):
    return [jax.ShapeDtypeStruct((n, LEV, BLOCK), F32) for n in (3 + side, 2, 2, side)]


def first_kernel(send_list, order, field_ref, *sends, side):
    fill_sends(sends, send_list, order, lambda b: block_at(field_ref, b), side)


def first_sends(field, send_list, order, side):
    return pl.pallas_call(
        functools.partial(first_kernel, side=side),
        in_specs=[SMEM, SMEM, VMEM],
        out_specs=[VMEM] * 4,
        out_shape=send_shapes(side),
        compiler_params=PARAMS,
        name="first_sends",
    )(send_list, order, field)


UNROLL = 6
SOLVED = 8


def own_kernel(pattern, *refs, own, targets, width, first, scale, flux):
    if flux:
        source_ref, edge_ref, start_ref, w_ref, out_ref, ext, wbuf, sems = refs
    else:
        source_ref, start_ref, w_ref, out_ref, ext, wbuf, sems = refs
    groups, size = targets // UNROLL, UNROLL * width

    def fetch(i):
        return pltpu.make_async_copy(w_ref.at[pl.ds(first + i * size, size)], wbuf.at[i], sems.at[i])

    for i in range(groups):
        fetch(i).start()

    def fill(b, _):
        x = block_at(source_ref, b)
        if flux:
            x = (x / SUBSTEPS) * edge_ref[b]
        store_parts(ext, b, x)
        return 0

    lax.fori_loop(0, own, fill, 0, unroll=4)
    ext[own] = jnp.zeros((2 * LEV, BLOCK), BF)

    def some(i, _):
        fetch(i).wait()
        for j in range(UNROLL):
            t = i * UNROLL + j
            x = jnp.concatenate([ext[jnp.minimum(pattern[t * width + k], own)] for k in range(width)], axis=1)
            w = wbuf[i, j * width : (j + 1) * width].reshape(width * BLOCK, 2 * BLOCK)
            y = jnp.dot(x, w, preferred_element_type=F32)
            out_ref[:, columns(t)] = block_at(start_ref, t) - scale * summed(y)
        return 0

    lax.fori_loop(0, groups, some, 0)


def own_product(pattern, source, start, weights, own, targets, width, first, scale, edge=None):
    ins = [source] + ([] if edge is None else [edge]) + [start, weights]
    return pl.pallas_call(
        functools.partial(own_kernel, own=own, targets=targets, width=width, first=first, scale=scale, flux=edge is not None),
        in_specs=[SMEM] + [VMEM] * (len(ins) - 1) + [HBM],
        out_specs=VMEM,
        out_shape=jax.ShapeDtypeStruct(start.shape, F32),
        scratch_shapes=[
            pltpu.VMEM((own + 1, 2 * LEV, BLOCK), BF),
            pltpu.VMEM((targets // UNROLL, UNROLL * width, BLOCK, 2 * BLOCK), BF),
            pltpu.SemaphoreType.DMA((targets // UNROLL,)),
        ],
        compiler_params=BIG,
        cost_estimate=cost(0, 1 << 18),
        name="own_product",
    )(pattern, *ins)


def rim_kernel(slot, target, count, *refs, targets, side, next_side, first, scale, flux, solve):
    refs = list(refs)
    held = At(refs.pop(0), STARTS["edge_held"]) if flux else None
    if next_side:
        send_list, order = refs.pop(0), refs.pop(0)
    partial_ref, w_ref = refs.pop(0), refs.pop(0)
    rim, refs = refs[:5], refs[5:]
    edge_ref = refs.pop(0) if flux else None
    inv_ref = refs.pop(0) if solve else None
    out_ref = refs.pop(0)
    sends, refs = (refs[:4], refs[4:]) if next_side else ((), refs)
    ext, wbuf, sems = refs.pop(0), refs.pop(0), refs.pop(0)
    acc = refs.pop(0) if solve else out_ref

    def fetch(g):
        return pltpu.make_async_copy(w_ref.at[pl.ds(first + g * GROUP, GROUP)], wbuf.at[pl.ds(g * GROUP, GROUP)], sems.at[g])

    def begin(g, _):
        fetch(g).start()
        return 0

    lax.fori_loop(0, count[0], begin, 0)
    for j, ref, i in rim_blocks(rim, side):
        x = ref[i]
        if flux:
            x = (x / SUBSTEPS) * edge_ref[held[NE + j]]
        store_parts(ext, j, x)
    ext[LAT - 1] = jnp.zeros((2 * LEV, BLOCK), BF)
    acc[...] = partial_ref[...]

    def some(i, _):
        at = i * GROUP
        parts = []
        fetch(i).wait()
        for j in range(GROUP):
            y = jnp.dot(ext[slot[at + j]], wbuf[at + j], preferred_element_type=F32)
            parts.append(scale * summed(y))
        for j in range(GROUP):
            t = target[at + j]
            acc[:, columns(t)] = block_at(acc, t) - parts[j]
        return 0

    lax.fori_loop(0, count[0], some, 0)

    if solve:
        def solved(i, _):
            for j in range(SOLVED):
                b = i * SOLVED + j
                p_hi, p_lo = two_parts(block_at(acc, b))
                y = jnp.dot(inv_ref[b], jnp.concatenate([p_hi, p_lo], axis=1), preferred_element_type=F32)
                out_ref[:, columns(b)] = summed(y)
            return 0

        lax.fori_loop(0, targets // SOLVED, solved, 0)
    if next_side:
        fill_sends(sends, send_list, order, lambda b: block_at(out_ref, b), next_side)


def rim_product(lists, partial, weights, rim, targets, side, scale, sends=None, next_side=0, edge=None, held=None, inverse=None):
    ins = [partial, weights, *rim]
    if edge is not None:
        ins.append(edge)
    if inverse is not None:
        ins.append(inverse)
    scalars = [*lists] + ([] if edge is None else [held]) + ([] if sends is None else [*sends])
    out_shape = [jax.ShapeDtypeStruct(partial.shape, F32)] + (send_shapes(next_side) if next_side else [])
    rim_terms = G_RIM if targets == NE else D_RIM
    scratch = [
        pltpu.VMEM((LAT + 2 * side, 2 * LEV, BLOCK), BF),
        pltpu.VMEM((rim_terms, BLOCK, 2 * BLOCK), BF),
        pltpu.SemaphoreType.DMA((rim_terms // GROUP,)),
    ]
    if inverse is not None:
        scratch.append(pltpu.VMEM(partial.shape, F32))
    out = pl.pallas_call(
        functools.partial(
            rim_kernel, targets=targets, side=side, next_side=next_side, first=G_AT if targets == NE else D_AT, scale=scale, flux=edge is not None, solve=inverse is not None
        ),
        in_specs=[SMEM] * len(scalars) + [VMEM, HBM] + [VMEM] * (len(ins) - 2),
        out_specs=[VMEM] * len(out_shape),
        out_shape=out_shape,
        scratch_shapes=scratch,
        compiler_params=BIG,
        cost_estimate=cost(1 << 30, 4 << 20),
        name="rim_product",
    )(*scalars, *ins)
    return out[0], out[1:]


ROWS_AT_ONCE = 32
PARTS = (8, 8, 8, 8, 8, 8, 4)


def turned(x):
    return jnp.transpose(x, (1, 0))


def table_kernel(info, tracer_ref, *refs):
    held = At(info, STARTS["wide_held"])
    rim, table_ref = refs[:5], refs[5]

    def put(slot, x):
        padded = jnp.concatenate([x, jnp.zeros((BLOCK - LEV, BLOCK), F32)], axis=0)
        table_ref[columns(slot), :] = turned(padded)

    def one(b, _):
        put(b, block_at(tracer_ref, b))
        return 0

    lax.fori_loop(0, NB, one, 0, unroll=2)
    for j, ref, i in rim_blocks(rim, WR):
        put(held[NB + j], ref[i])
    put(held[NB + LAT - 1], jnp.zeros((LEV, BLOCK), F32))


def tracer_table(held, tracer, rim):
    cells = (NB + LAT + 2 * WR) * BLOCK
    return pl.pallas_call(
        table_kernel,
        in_specs=[SMEM] + [VMEM] * 6,
        out_specs=VMEM,
        out_shape=jax.ShapeDtypeStruct((cells, BLOCK), F32),
        compiler_params=PARAMS,
        cost_estimate=cost(0, 1 << 18),
        name="tracer_table",
    )(held, tracer, *rim)


def cells_by_part(edge_cells):
    at, parts = 0, []
    for blocks in PARTS:
        parts.append(edge_cells[:, at * BLOCK : (at + blocks) * BLOCK].reshape(-1))
        at += blocks
    return jnp.concatenate(parts)


def edge_tracer_kernel(cells_ref, table_ref, out_ref, rows, cells, sem, *, start, blocks):
    count = blocks * BLOCK
    fetch = pltpu.make_async_copy(cells_ref.at[pl.ds(2 * start * BLOCK, 2 * count)], cells, sem)
    fetch.start()
    fetch.wait()

    def block(e, _):
        def some(i, _):
            at = e * BLOCK + i * ROWS_AT_ONCE
            sums = []
            for j in range(ROWS_AT_ONCE):
                a = table_ref[pl.ds(cells[at + j], 1), :]
                b = table_ref[pl.ds(cells[count + at + j], 1), :]
                sums.append(a + b)
            for j in range(ROWS_AT_ONCE):
                rows[pl.ds(i * ROWS_AT_ONCE + j, 1), :] = sums[j]
            return 0

        lax.fori_loop(0, BLOCK // ROWS_AT_ONCE, some, 0)
        out_ref[e] = 0.5 * turned(rows[...])[:LEV]
        return 0

    lax.fori_loop(0, blocks, block, 0)


def edge_tracer_part(table, cells, start, blocks):
    return pl.pallas_call(
        functools.partial(edge_tracer_kernel, start=start, blocks=blocks),
        in_specs=[HBM, VMEM],
        out_specs=VMEM,
        out_shape=jax.ShapeDtypeStruct((blocks, LEV, BLOCK), F32),
        scratch_shapes=[
            pltpu.VMEM((BLOCK, BLOCK), F32),
            pltpu.SMEM((2 * blocks * BLOCK,), jnp.int32),
            pltpu.SemaphoreType.DMA,
        ],
        compiler_params=PARAMS,
        cost_estimate=cost(0, 1 << 18),
        name="edge_tracer",
    )(cells, table)


def together(*xs):
    return lax.optimization_barrier(xs)


def body(
    mass_field,
    normal_wind,
    tracer_ratio,
    gradient_weights,
    divergence_weights,
    vertical_inverse,
    gradient_pattern,
    divergence_pattern,
    edge_cells,
    cell_sends,
    edge_sends,
    wide_sends,
):
    info = row_of_tables()
    cell_list, edge_list, wide_list = cell_sends[0], edge_sends[0], wide_sends[0]
    g_pattern = gradient_pattern.reshape(-1)
    d_pattern = divergence_pattern.reshape(-1)


    def g_own(mass, wind):
        return own_product(g_pattern, mass, wind, weights, NB, NE, KG, 0, time_step)

    def d_own(source, start, scale, edge=None):
        return own_product(d_pattern, source, start, weights, NE, NB, KD, G_TERMS, scale, edge)

    def prepared(g_weights):
        nonlocal weights
        weights, *lists = split_weights(g_pattern, d_pattern, info, g_weights, divergence_weights)
        return g_own(mass_field, normal_wind), split_inverse(vertical_inverse), lists, cells_by_part(edge_cells)

    weights = None
    first = first_sends(mass_field, cell_list, info, SR)
    wide = first_sends(tracer_ratio, wide_list, info, WR)
    pre_in, wide_pre_in, g_weights = together(hand_over(first), hand_over(wide), gradient_weights)
    (partial, inverse, lists, cells), rim = travel(first, pre_in, prepared, g_weights)
    g_terms, d_terms = lists[:3], lists[3:]
    tracer_rim = travel(wide, wide_pre_in, lambda: ())[1]
    edge_parts = []
    table = None

    def tracer_work(window, partial):
        nonlocal table
        if window == 1:
            partial, *rim = together(partial, *tracer_rim)
            table = tracer_table(info, tracer_ratio, rim)
            partial, table = together(partial, table)
        elif window - 2 < len(PARTS):
            blocks, start = PARTS[window - 2], sum(PARTS[: window - 2])
            partial, now = together(partial, table)
            part = edge_tracer_part(now, cells, start, blocks)
            partial, part = together(partial, part)
            edge_parts.append(part)
        return partial

    mass, wind = mass_field, normal_wind
    winds, rims = [], []
    for substep in range(SUBSTEPS):
        if substep > 0:
            partial, rim = exchange(sends, lambda m, w: tracer_work(2 * substep, g_own(m, w)), mass, wind)
        wind, sends = rim_product(g_terms, partial, weights, rim, NE, SR, time_step, (edge_list, info), ER)
        winds.append(wind)
        if substep < SUBSTEPS - 1:
            partial, rim = exchange(sends, lambda w, m: tracer_work(2 * substep + 1, d_own(w, m, time_step)), wind, mass)
        else:

            def last_work(w, m, *earlier):
                edge_tracer = jnp.concatenate(edge_parts, axis=0)
                total = functools.reduce(jnp.add, (*earlier, w))
                partial, total, tracer = together(d_own(w, m, time_step), total, tracer_ratio)
                return partial, d_own(total, tracer, tracer_step, edge_tracer), edge_tracer

            (partial, t_partial, edge_tracer), rim = exchange(sends, last_work, wind, mass, *winds[:-1])
        rims.append(rim)
        if substep < SUBSTEPS - 1:
            mass, sends = rim_product(d_terms, partial, weights, rim, NB, ER, time_step, (cell_list, info), SR, inverse=inverse)
        else:
            mass, _ = rim_product(d_terms, partial, weights, rim, NB, ER, time_step, inverse=inverse)
    total_rim = [functools.reduce(jnp.add, parts) for parts in zip(*rims)]
    tracer_final, _ = rim_product(d_terms, t_partial, weights, total_rim, NB, ER, tracer_step, edge=edge_tracer, held=info)
    return mass, wind, tracer_final


def solution(mesh):
    both = ("region", "sub")
    return jax.shard_map(
        body,
        mesh=mesh,
        in_specs=(
            P(None, both),
            P(None, both),
            P(None, both),
            P(both, None, None, None),
            P(both, None, None, None),
            P(both, None, None),
            P(both, None),
            P(both, None),
            P(None, both),
            P(both, None),
            P(both, None),
            P(both, None),
        ),
        out_specs=(P(None, both), P(None, both), P(None, both)),
        check_vma=False,
    )
```

```python
import functools

import numpy as np
import jax
import jax.numpy as jnp
from jax import lax
from jax.experimental import pallas as pl
from jax.experimental.pallas import tpu as pltpu
from jax.sharding import PartitionSpec as P

BLOCK = 128
LEV = 96
NB = 24
NE = 36
KG = 3
KD = 4
SR = 4
ER = 4
WR = 8
SUBSTEPS = 5
N_REGION = 16
N_CHIP = 4
N_SUB = 8
LAT = 8

time_step = 0.25
tracer_step = 0.5

BF = jnp.bfloat16
F32 = jnp.float32

ALONG = [(2 * x + c, 2 * ((x + (1 if c == 0 else 3)) % 4) + c) for x in range(4) for c in range(2)]
ACROSS = [(2 * x + c, 2 * ((x + 2) % 4) + c) for x in range(4) for c in range(2)]
MATES = [(s, s ^ 1) for s in range(8)]
REGIONS = [(r * 8 + s, (r + (1 if s % 2 == 0 else 15)) % 16 * 8 + s) for r in range(16) for s in range(8)]


def send_order(side):
    rows = []
    for s in range(N_SUB):
        x, c = divmod(s, 2)
        mine = (x + (1 if c == 0 else 3)) % 4
        other = (x + (3 if c == 0 else 1)) % 4
        far = (x + 2) % 4
        o = 1 - c
        to_next = [LAT + j for j in range(side)]
        to_prev = [LAT + side + j for j in range(side)]
        kept, given = (to_next, to_prev) if c == 0 else (to_prev, to_next)
        rows.append(
            [2 * x + o, 2 * other + o, 2 * other + c, *given]
            + [2 * mine + c, 2 * mine + o, 2 * far + c, 2 * far + o, *kept]
        )
    return np.array(rows, np.int32)


def lateral_place():
    rows = []
    for s in range(N_SUB):
        x, c = divmod(s, 2)
        back = 3 if c == 0 else 1
        row = []
        for p in range(N_SUB):
            px, pc = divmod(p, 2)
            d = (px - x) % 4
            same = pc == c
            if d == 0:
                row.append(7 if same else 0)
            elif d == back:
                row.append(1 if same else 2)
            elif d == 2:
                row.append(3 if same else 6)
            else:
                row.append(5 if same else 4)
        rows.append(row)
    return np.array(rows, np.int32)


def place_table(own, side):
    lat = lateral_place()
    rows = []
    for s in range(N_SUB):
        first, second = np.arange(side), side + np.arange(side)
        prev, nxt = (first, second) if s % 2 == 0 else (second, first)
        rows.append(np.concatenate([np.arange(own), own + lat[s], own + LAT + prev, own + LAT + nxt]))
    return np.stack(rows).astype(np.int32)


def held_table(own, side):
    return np.argsort(place_table(own, side), axis=1).astype(np.int32)


class At:
    def __init__(self, ref, start):
        self.ref, self.start = ref, start

    def __getitem__(self, i):
        return self.ref[self.start + i]


def all_tables():
    tables = dict(
        order=send_order(SR),
        wide_order=send_order(WR),
        cell_place=place_table(NB, SR),
        edge_place=place_table(NE, ER),
        wide_held=held_table(NB, WR),
        edge_held=held_table(NE, ER),
    )
    starts, at = {}, 0
    for name, table in tables.items():
        starts[name] = at
        at += table.shape[1]
    return np.concatenate(list(tables.values()), axis=1), starts


TABLES, STARTS = all_tables()


def row_of_tables():
    sub = lax.axis_index("sub")
    return lax.dynamic_slice(jnp.asarray(TABLES), (sub, 0), (1, TABLES.shape[1]))[0]


def hand_over(sends):
    return lax.ppermute(sends[0], "sub", MATES)


def exchange(sends, work, *given):
    pre_in, *given = together(hand_over(sends), *given)
    return travel(sends, pre_in, work, *given)


def travel(sends, pre_in, work, *given):
    _, along, across, region = sends
    region_in = lax.ppermute(jnp.concatenate([region, pre_in[3:]], axis=0), ("region", "sub"), REGIONS)
    along_in = lax.ppermute(jnp.concatenate([along, pre_in[1:3]], axis=0), "sub", ALONG)
    across_in = lax.ppermute(across, "sub", ACROSS)
    side = region.shape[0]
    done, along_in, across_in, region_in = together(work(*given), along_in, across_in, region_in)
    post = jnp.concatenate([along_in[1:2], along_in[3:4], across_in[1:2], region_in[side:]], axis=0)
    post_in = lax.ppermute(post, "sub", MATES)
    return done, (pre_in, along_in, across_in, region_in, post_in)


def two_parts(x):
    hi = x.astype(BF)
    lo = (x - hi.astype(F32)).astype(BF)
    return hi, lo


VMEM = pl.BlockSpec(memory_space=pltpu.VMEM)
SMEM = pl.BlockSpec(memory_space=pltpu.SMEM)
HBM = pl.BlockSpec(memory_space=pltpu.HBM)
PARAMS = pltpu.CompilerParams(vmem_limit_bytes=16 << 20)
BIG = pltpu.CompilerParams(vmem_limit_bytes=40 << 20)
BIGGEST = pltpu.CompilerParams(vmem_limit_bytes=58 << 20)


def cost(flops, moved):
    return pl.CostEstimate(flops=flops, bytes_accessed=moved, transcendentals=0)


GROUP = 8
ROOM = 128
CUT = 12
READS = 6
G_TERMS = NE * KG
D_TERMS = NB * KD
G_RIM = NE * (KG - 1) + GROUP
D_RIM = D_TERMS + GROUP
G_AT = G_TERMS + D_TERMS
D_AT = G_AT + G_RIM
ALL_TERMS = D_AT + D_RIM


def split_kernel(g_pattern, d_pattern, info, g_ref, d_ref, out_ref, g_slot, g_target, g_count, d_slot, d_target, d_count, raw, cut, rim, in_sem, out_sem, rim_sem):
    g_steps, d_steps = G_TERMS // CUT, D_TERMS // CUT
    steps = g_steps + d_steps

    def read(i):
        ref, j = (g_ref, i) if i < g_steps else (d_ref, i - g_steps)
        return pltpu.make_async_copy(ref.at[pl.ds(j * CUT, CUT)], raw.at[i % READS], in_sem.at[i])

    def write(i):
        return pltpu.make_async_copy(cut.at[i], out_ref.at[pl.ds(i * CUT, CUT)], out_sem.at[i])

    def write_rim(at, g):
        rows = pl.ds(at + g * GROUP, GROUP)
        return pltpu.make_async_copy(rim.at[rows], out_ref.at[pl.ds(at + G_AT + g * GROUP, GROUP)], rim_sem.at[at // GROUP + g])

    def finish(at, n, slot, target, count):
        for j in range(GROUP):
            rim[n + j] = jnp.zeros((BLOCK, 2 * BLOCK), BF)
            slot[n - at + j] = LAT - 1
            target[n - at + j] = 0
        groups = (n - at + GROUP - 1) // GROUP
        count[0] = groups

        def one(g, _):
            write_rim(at, g).start()
            return 0

        lax.fori_loop(0, groups, one, 0)
        return groups

    for i in range(READS):
        read(i).start()
    n = jnp.int32(0)
    for i in range(steps):
        read(i).wait()
        if i < g_steps:
            pattern, own, start, at, width, lists = g_pattern, NB, i * CUT, 0, KG, (g_slot, g_target)
            place = At(info, STARTS["cell_place"])
        else:
            pattern, own, start, at, width, lists = d_pattern, NE, (i - g_steps) * CUT, G_RIM, KD, (d_slot, d_target)
            place = At(info, STARTS["edge_place"])
        if i == g_steps:
            g_groups = finish(0, n, g_slot, g_target, g_count)
            n = jnp.int32(G_RIM)

        def one(j, n):
            hi, lo = two_parts(raw[i % READS, j])
            both = jnp.concatenate([hi, lo], axis=1)
            cut[i, j] = both
            rim[n] = both
            e = pattern[start + j]
            slot, target = lists
            slot[n - at] = place[e] - own
            target[n - at] = start // width + (j * 43 >> 7 if width == 3 else j >> 2)
            return n + (e >= own).astype(jnp.int32)

        n = lax.fori_loop(0, CUT, one, n, unroll=4)
        write(i).start()
        if i + READS < steps:
            read(i + READS).start()
    d_groups = finish(G_RIM, n, d_slot, d_target, d_count)
    for i in range(steps):
        write(i).wait()
    for at, groups in ((0, g_groups), (G_RIM, d_groups)):

        def done(g, _, at=at):
            write_rim(at, g).wait()
            return 0

        lax.fori_loop(0, groups, done, 0)


def split_weights(g_pattern, d_pattern, info, g, d):
    steps = (G_TERMS + D_TERMS) // CUT
    return pl.pallas_call(
        split_kernel,
        in_specs=[SMEM] * 3 + [HBM] * 2,
        out_specs=[HBM] + [SMEM] * 6,
        out_shape=[jax.ShapeDtypeStruct((ALL_TERMS, BLOCK, 2 * BLOCK), BF)]
        + [jax.ShapeDtypeStruct((n,), jnp.int32) for n in (ROOM, ROOM, 1)] * 2,
        scratch_shapes=[
            pltpu.VMEM((READS, CUT, BLOCK, BLOCK), F32),
            pltpu.VMEM((steps, CUT, BLOCK, 2 * BLOCK), BF),
            pltpu.VMEM((G_RIM + D_RIM, BLOCK, 2 * BLOCK), BF),
            pltpu.SemaphoreType.DMA((steps,)),
            pltpu.SemaphoreType.DMA((steps,)),
            pltpu.SemaphoreType.DMA(((G_RIM + D_RIM) // GROUP,)),
        ],
        compiler_params=BIGGEST,
        cost_estimate=cost(0, 30 << 20),
        name="split_weights",
    )(g_pattern, d_pattern, info, g.reshape(-1, BLOCK, BLOCK), d.reshape(-1, BLOCK, BLOCK))


def split_inverse_kernel(v_ref, o_ref):
    hi, lo = two_parts(v_ref[...])
    o_ref[:, :LEV] = hi
    o_ref[:, LEV:] = lo


def split_inverse(inverse):
    return pl.pallas_call(
        split_inverse_kernel,
        grid=(4,),
        in_specs=[pl.BlockSpec((NB // 4, LEV, LEV), lambda i: (i, 0, 0))],
        out_specs=pl.BlockSpec((NB // 4, 2 * LEV, LEV), lambda i: (i, 0, 0)),
        out_shape=jax.ShapeDtypeStruct((NB, 2 * LEV, LEV), BF),
        compiler_params=PARAMS,
        cost_estimate=cost(NB * LEV * LEV * 4, NB * LEV * LEV * 8),
        name="split_inverse",
    )(inverse)


RIM = ((0, 0), (1, 0), (1, 2), (2, 0), (4, 0), (4, 1), (4, 2))


def rim_blocks(rim, side):
    blocks = [(j, rim[which], i) for j, (which, i) in enumerate(RIM)]
    blocks += [(LAT + i, rim[3], i) for i in range(side)]
    blocks += [(LAT + side + i, rim[4], 3 + i) for i in range(side)]
    return blocks


def store_parts(ext, slot, x):
    hi, lo = two_parts(x)
    ext[slot, :LEV, :] = hi
    ext[slot, LEV:, :] = lo


def columns(b):
    return pl.ds(b * BLOCK if isinstance(b, int) else pl.multiple_of(b * BLOCK, BLOCK), BLOCK)


def block_at(ref, b):
    return ref[:, columns(b)]


def summed(y):
    return (y[:LEV, :BLOCK] + y[LEV:, :BLOCK]) + (y[:LEV, BLOCK:] + y[LEV:, BLOCK:])


def pick(source, entry):
    live = (entry >= 0).astype(F32)
    return source(jnp.maximum(entry, 0)) * live


def fill_sends(sends, send_list, info, source, side):
    order = At(info, STARTS["order" if side == SR else "wide_order"])
    at = 0
    for ref, n in zip(sends, (3 + side, 2, 2, side)):
        for j in range(n):
            ref[j] = pick(source, send_list[order[at + j]])
        at += n


def send_shapes(side):
    return [jax.ShapeDtypeStruct((n, LEV, BLOCK), F32) for n in (3 + side, 2, 2, side)]


def first_kernel(send_list, order, field_ref, *sends, side):
    fill_sends(sends, send_list, order, lambda b: block_at(field_ref, b), side)


def first_sends(field, send_list, order, side):
    return pl.pallas_call(
        functools.partial(first_kernel, side=side),
        in_specs=[SMEM, SMEM, VMEM],
        out_specs=[VMEM] * 4,
        out_shape=send_shapes(side),
        compiler_params=PARAMS,
        name="first_sends",
    )(send_list, order, field)


UNROLL = 6
SOLVED = 8


def own_kernel(pattern, *refs, own, targets, width, first, scale, flux):
    if flux:
        source_ref, edge_ref, start_ref, w_ref, out_ref, ext, wbuf, sems = refs
    else:
        source_ref, start_ref, w_ref, out_ref, ext, wbuf, sems = refs
    groups, size = targets // UNROLL, UNROLL * width

    def fetch(i):
        return pltpu.make_async_copy(w_ref.at[pl.ds(first + i * size, size)], wbuf.at[i], sems.at[i])

    for i in range(groups):
        fetch(i).start()

    def fill(b, _):
        x = block_at(source_ref, b)
        if flux:
            x = (x / SUBSTEPS) * edge_ref[b]
        store_parts(ext, b, x)
        return 0

    lax.fori_loop(0, own, fill, 0, unroll=4)
    ext[own] = jnp.zeros((2 * LEV, BLOCK), BF)

    def some(i, _):
        fetch(i).wait()
        for j in range(UNROLL):
            t = i * UNROLL + j
            x = jnp.concatenate([ext[jnp.minimum(pattern[t * width + k], own)] for k in range(width)], axis=1)
            w = wbuf[i, j * width : (j + 1) * width].reshape(width * BLOCK, 2 * BLOCK)
            y = jnp.dot(x, w, preferred_element_type=F32)
            out_ref[:, columns(t)] = block_at(start_ref, t) - scale * summed(y)
        return 0

    lax.fori_loop(0, groups, some, 0)


def own_product(pattern, source, start, weights, own, targets, width, first, scale, edge=None):
    ins = [source] + ([] if edge is None else [edge]) + [start, weights]
    return pl.pallas_call(
        functools.partial(own_kernel, own=own, targets=targets, width=width, first=first, scale=scale, flux=edge is not None),
        in_specs=[SMEM] + [VMEM] * (len(ins) - 1) + [HBM],
        out_specs=VMEM,
        out_shape=jax.ShapeDtypeStruct(start.shape, F32),
        scratch_shapes=[
            pltpu.VMEM((own + 1, 2 * LEV, BLOCK), BF),
            pltpu.VMEM((targets // UNROLL, UNROLL * width, BLOCK, 2 * BLOCK), BF),
            pltpu.SemaphoreType.DMA((targets // UNROLL,)),
        ],
        compiler_params=BIG,
        cost_estimate=cost(0, 1 << 18),
        name="own_product",
    )(pattern, *ins)


def rim_kernel(slot, target, count, *refs, targets, side, next_side, first, scale, flux, solve):
    refs = list(refs)
    held = At(refs.pop(0), STARTS["edge_held"]) if flux else None
    if next_side:
        send_list, order = refs.pop(0), refs.pop(0)
    partial_ref, w_ref = refs.pop(0), refs.pop(0)
    rim, refs = refs[:5], refs[5:]
    edge_ref = refs.pop(0) if flux else None
    inv_ref = refs.pop(0) if solve else None
    out_ref = refs.pop(0)
    sends, refs = (refs[:4], refs[4:]) if next_side else ((), refs)
    ext, wbuf, sems = refs.pop(0), refs.pop(0), refs.pop(0)
    acc = refs.pop(0) if solve else out_ref

    def fetch(g):
        return pltpu.make_async_copy(w_ref.at[pl.ds(first + g * GROUP, GROUP)], wbuf.at[pl.ds(g * GROUP, GROUP)], sems.at[g])

    def begin(g, _):
        fetch(g).start()
        return 0

    lax.fori_loop(0, count[0], begin, 0)
    for j, ref, i in rim_blocks(rim, side):
        x = ref[i]
        if flux:
            x = (x / SUBSTEPS) * edge_ref[held[NE + j]]
        store_parts(ext, j, x)
    ext[LAT - 1] = jnp.zeros((2 * LEV, BLOCK), BF)
    acc[...] = partial_ref[...]

    def some(i, _):
        at = i * GROUP
        parts = []
        fetch(i).wait()
        for j in range(GROUP):
            y = jnp.dot(ext[slot[at + j]], wbuf[at + j], preferred_element_type=F32)
            parts.append(scale * summed(y))
        for j in range(GROUP):
            t = target[at + j]
            acc[:, columns(t)] = block_at(acc, t) - parts[j]
        return 0

    lax.fori_loop(0, count[0], some, 0)

    if solve:
        def solved(i, _):
            for j in range(SOLVED):
                b = i * SOLVED + j
                p_hi, p_lo = two_parts(block_at(acc, b))
                y = jnp.dot(inv_ref[b], jnp.concatenate([p_hi, p_lo], axis=1), preferred_element_type=F32)
                out_ref[:, columns(b)] = summed(y)
            return 0

        lax.fori_loop(0, targets // SOLVED, solved, 0)
    if next_side:
        fill_sends(sends, send_list, order, lambda b: block_at(out_ref, b), next_side)


def rim_product(lists, partial, weights, rim, targets, side, scale, sends=None, next_side=0, edge=None, held=None, inverse=None):
    ins = [partial, weights, *rim]
    if edge is not None:
        ins.append(edge)
    if inverse is not None:
        ins.append(inverse)
    scalars = [*lists] + ([] if edge is None else [held]) + ([] if sends is None else [*sends])
    out_shape = [jax.ShapeDtypeStruct(partial.shape, F32)] + (send_shapes(next_side) if next_side else [])
    rim_terms = G_RIM if targets == NE else D_RIM
    scratch = [
        pltpu.VMEM((LAT + 2 * side, 2 * LEV, BLOCK), BF),
        pltpu.VMEM((rim_terms, BLOCK, 2 * BLOCK), BF),
        pltpu.SemaphoreType.DMA((rim_terms // GROUP,)),
    ]
    if inverse is not None:
        scratch.append(pltpu.VMEM(partial.shape, F32))
    out = pl.pallas_call(
        functools.partial(
            rim_kernel, targets=targets, side=side, next_side=next_side, first=G_AT if targets == NE else D_AT, scale=scale, flux=edge is not None, solve=inverse is not None
        ),
        in_specs=[SMEM] * len(scalars) + [VMEM, HBM] + [VMEM] * (len(ins) - 2),
        out_specs=[VMEM] * len(out_shape),
        out_shape=out_shape,
        scratch_shapes=scratch,
        compiler_params=BIG,
        cost_estimate=cost(1 << 30, 4 << 20),
        name="rim_product",
    )(*scalars, *ins)
    return out[0], out[1:]


ROWS_AT_ONCE = 32
PARTS = (8, 8, 8, 8, 8, 8, 4)


def turned(x):
    return jnp.transpose(x, (1, 0))


def table_kernel(info, tracer_ref, *refs):
    held = At(info, STARTS["wide_held"])
    rim, table_ref = refs[:5], refs[5]

    def put(slot, x):
        padded = jnp.concatenate([x, jnp.zeros((BLOCK - LEV, BLOCK), F32)], axis=0)
        table_ref[columns(slot), :] = turned(padded)

    def one(b, _):
        put(b, block_at(tracer_ref, b))
        return 0

    lax.fori_loop(0, NB, one, 0, unroll=2)
    for j, ref, i in rim_blocks(rim, WR):
        put(held[NB + j], ref[i])
    put(held[NB + LAT - 1], jnp.zeros((LEV, BLOCK), F32))


def tracer_table(held, tracer, rim):
    cells = (NB + LAT + 2 * WR) * BLOCK
    return pl.pallas_call(
        table_kernel,
        in_specs=[SMEM] + [VMEM] * 6,
        out_specs=VMEM,
        out_shape=jax.ShapeDtypeStruct((cells, BLOCK), F32),
        compiler_params=PARAMS,
        cost_estimate=cost(0, 1 << 18),
        name="tracer_table",
    )(held, tracer, *rim)


def cells_by_part(edge_cells):
    at, parts = 0, []
    for blocks in PARTS:
        parts.append(edge_cells[:, at * BLOCK : (at + blocks) * BLOCK].reshape(-1))
        at += blocks
    return jnp.concatenate(parts)


def edge_tracer_kernel(cells_ref, table_ref, out_ref, rows, cells, sem, *, start, blocks):
    count = blocks * BLOCK
    fetch = pltpu.make_async_copy(cells_ref.at[pl.ds(2 * start * BLOCK, 2 * count)], cells, sem)
    fetch.start()
    fetch.wait()

    def block(e, _):
        def some(i, _):
            at = e * BLOCK + i * ROWS_AT_ONCE
            sums = []
            for j in range(ROWS_AT_ONCE):
                a = table_ref[pl.ds(cells[at + j], 1), :]
                b = table_ref[pl.ds(cells[count + at + j], 1), :]
                sums.append(a + b)
            for j in range(ROWS_AT_ONCE):
                rows[pl.ds(i * ROWS_AT_ONCE + j, 1), :] = sums[j]
            return 0

        lax.fori_loop(0, BLOCK // ROWS_AT_ONCE, some, 0)
        out_ref[e] = 0.5 * turned(rows[...])[:LEV]
        return 0

    lax.fori_loop(0, blocks, block, 0)


def edge_tracer_part(table, cells, start, blocks):
    return pl.pallas_call(
        functools.partial(edge_tracer_kernel, start=start, blocks=blocks),
        in_specs=[HBM, VMEM],
        out_specs=VMEM,
        out_shape=jax.ShapeDtypeStruct((blocks, LEV, BLOCK), F32),
        scratch_shapes=[
            pltpu.VMEM((BLOCK, BLOCK), F32),
            pltpu.SMEM((2 * blocks * BLOCK,), jnp.int32),
            pltpu.SemaphoreType.DMA,
        ],
        compiler_params=PARAMS,
        cost_estimate=cost(0, 1 << 18),
        name="edge_tracer",
    )(cells, table)


def together(*xs):
    return lax.optimization_barrier(xs)


def body(
    mass_field,
    normal_wind,
    tracer_ratio,
    gradient_weights,
    divergence_weights,
    vertical_inverse,
    gradient_pattern,
    divergence_pattern,
    edge_cells,
    cell_sends,
    edge_sends,
    wide_sends,
):
    info = row_of_tables()
    cell_list, edge_list, wide_list = cell_sends[0], edge_sends[0], wide_sends[0]
    g_pattern = gradient_pattern.reshape(-1)
    d_pattern = divergence_pattern.reshape(-1)


    def g_own(mass, wind):
        return own_product(g_pattern, mass, wind, weights, NB, NE, KG, 0, time_step)

    def d_own(source, start, scale, edge=None):
        return own_product(d_pattern, source, start, weights, NE, NB, KD, G_TERMS, scale, edge)

    def prepared(g_weights):
        nonlocal weights
        weights, *lists = split_weights(g_pattern, d_pattern, info, g_weights, divergence_weights)
        return g_own(mass_field, normal_wind), split_inverse(vertical_inverse), lists, cells_by_part(edge_cells)

    weights = None
    first = first_sends(mass_field, cell_list, info, SR)
    wide = first_sends(tracer_ratio, wide_list, info, WR)
    pre_in, wide_pre_in, g_weights = together(hand_over(first), hand_over(wide), gradient_weights)
    (partial, inverse, lists, cells), rim = travel(first, pre_in, prepared, g_weights)
    g_terms, d_terms = lists[:3], lists[3:]
    tracer_rim = travel(wide, wide_pre_in, lambda: ())[1]
    edge_parts = []
    table = None

    def tracer_work(window, partial):
        nonlocal table
        if window == 1:
            partial, *rim = together(partial, *tracer_rim)
            table = tracer_table(info, tracer_ratio, rim)
            partial, table = together(partial, table)
        elif window - 2 < len(PARTS):
            blocks, start = PARTS[window - 2], sum(PARTS[: window - 2])
            partial, now = together(partial, table)
            part = edge_tracer_part(now, cells, start, blocks)
            partial, part = together(partial, part)
            edge_parts.append(part)
        return partial

    mass, wind = mass_field, normal_wind
    winds, rims = [], []
    for substep in range(SUBSTEPS):
        if substep > 0:
            partial, rim = exchange(sends, lambda m, w: tracer_work(2 * substep, g_own(m, w)), mass, wind)
        wind, sends = rim_product(g_terms, partial, weights, rim, NE, SR, time_step, (edge_list, info), ER)
        winds.append(wind)
        if substep < SUBSTEPS - 1:
            partial, rim = exchange(sends, lambda w, m: tracer_work(2 * substep + 1, d_own(w, m, time_step)), wind, mass)
        else:

            def last_work(w, m, *earlier):
                edge_tracer = jnp.concatenate(edge_parts, axis=0)
                total = functools.reduce(jnp.add, (*earlier, w))
                partial, total, tracer = together(d_own(w, m, time_step), total, tracer_ratio)
                return partial, d_own(total, tracer, tracer_step, edge_tracer), edge_tracer

            (partial, t_partial, edge_tracer), rim = exchange(sends, last_work, wind, mass, *winds[:-1])
        rims.append(rim)
        if substep < SUBSTEPS - 1:
            mass, sends = rim_product(d_terms, partial, weights, rim, NB, ER, time_step, (cell_list, info), SR, inverse=inverse)
        else:
            mass, _ = rim_product(d_terms, partial, weights, rim, NB, ER, time_step, inverse=inverse)
    total_rim = [functools.reduce(jnp.add, parts) for parts in zip(*rims)]
    tracer_final, _ = rim_product(d_terms, t_partial, weights, total_rim, NB, ER, tracer_step, edge=edge_tracer, held=info)
    return mass, wind, tracer_final


def solution(mesh):
    both = ("region", "sub")
    return jax.shard_map(
        body,
        mesh=mesh,
        in_specs=(
            P(None, both),
            P(None, both),
            P(None, both),
            P(both, None, None, None),
            P(both, None, None, None),
            P(both, None, None),
            P(both, None),
            P(both, None),
            P(None, both),
            P(both, None),
            P(both, None),
            P(both, None),
        ),
        out_specs=(P(None, both), P(None, both), P(None, both)),
        check_vma=False,
    )
```
